32 devices in a mesh: groups: 2 (over y), gx: 16 (over z, x, core).
Axes of the slice: x: 2, y: 2, z: 4, core: 2. Of those that a mesh axis runs over, the one named last changes fastest.
Arguments:
- tokens: bfloat16 [64, 7168], P(('groups', 'gx')), parts along dimension 0, may hold values from -6 to 6
- route_ids: int32 [64, 2], P('groups'), parts along dimension 0, may hold values from 0 to 7, all different within a row; in each aligned block of 32 rows (0 to 31, 32 to 63, ...) at most 32 rows name the same one
- route_gates: float32 [64, 2], P('groups'), parts along dimension 0, may hold values from 0.2 to 1
- dense_gate: bfloat16 [7168, 4864], P(None, 'gx'), may hold values from -0.0625 to 0.0625
- dense_up: bfloat16 [7168, 4864], P(None, 'gx'), may hold values from -0.0625 to 0.0625
- dense_down: bfloat16 [4864, 7168], P(None, 'gx'), may hold values from -0.078125 to 0.078125
- expert_gate: bfloat16 [7168, 32768], P(None, 'gx'), may hold values from -0.0625 to 0.0625
- expert_up: bfloat16 [7168, 32768], P(None, 'gx'), may hold values from -0.0625 to 0.0625
- expert_down: bfloat16 [32768, 7168], P('gx'), may hold values from -0.09375 to 0.09375
Outputs:
- layer_out: bfloat16 [64, 7168], P(('groups', 'gx')), parts along dimension 0
The draws below stay inside these ranges and needn't reach their ends.
There are 2 independent parts, one for each index of `groups`. The reference program is written for one: setup_inputs(seed, part) draws one part's arguments, and reference() takes and returns one part's arrays. A program takes and returns all parts, laid end to end along the dimension named above; an argument that names none is the same for every part. Nothing has to cross between parts.
Inputs may be any that keep to these rules, and one draw needn't show every extreme that they name: `route_ids`: the 2 experts of a token differ; each expert is named by at most 32 tokens, a bound that some block reaches.
All inputs are finite; a program needn't handle non-finite values.
Results may differ from the reference program's by a relative error of at most 0.0042.
Values may be sent and summed in bfloat16 or wider, within the bound.
No kernel may reach another device: no remote copies, remote signals or barrier semaphores. Data moves between devices by JAX's collectives and lax.ppermute only.
A program may use at most 192 MiB of HBM per device.

```python
import math
import jax
import jax.numpy as jnp
import numpy as np
from jax import lax

D = 7168
FFD = 4864
EH = 4096
EXPERTS = 8
TOP = 2
TOKENS = 32
CAP = 32
EXP_COLS = 32768


def shard_levels(stream_key, shape, split, smallest, high):
    level = 1.0
    for dim, blocks in split:
        heights = jax.random.uniform(jax.random.fold_in(jax.random.fold_in(stream_key, 6), dim), (blocks,), jnp.float32, smallest / len(split), high / len(split))
        level = level * jnp.repeat(jnp.exp(heights), shape[dim] // blocks).reshape((-1,) + (1,) * (len(shape) - 1 - dim))
    return level


def deal_out(stream_key, own, number, rows, number_of, top, bound, lean):
    order = jax.random.permutation(stream_key, number_of)
    heavy_load, usual = shares(number_of, rows * top, bound, lean, True), shares(number_of, rows * top, bound, lean, False)
    places = jnp.arange(number_of)

    def named(lengths, rotation):
        used = int((lengths > 0).sum())
        fixed = max(1, used // 4)
        moved = fixed + (places - fixed + rotation * (used - fixed)) % max(1, number_of - fixed)
        return jnp.zeros((number_of,), jnp.int32).at[order[jnp.where(places < fixed, places, moved)]].set(jnp.asarray(lengths, jnp.int32))

    lengths = jnp.where(number % 4 == 0, named(heavy_load, number // 4), named(usual, number - number // 4 - 1))
    mixed = jax.random.permutation(jax.random.fold_in(own, 3), number_of)
    source_of, taker = mixed[0:number_of // 2 * 2:2], mixed[1:number_of // 2 * 2:2]
    margin = jnp.minimum(lengths[source_of] - 1, bound - lengths[taker]) // 2
    margin = jnp.where((source_of == order[0]) | (taker == order[0]) | (lengths[taker] == 0), 0, jnp.maximum(margin, 0))
    moved = jax.random.randint(jax.random.fold_in(own, 4), (number_of // 2,), 0, 1 << 20) % (margin + 1)
    lengths = lengths.at[source_of].add(-moved).at[taker].add(moved)
    items = jnp.searchsorted(jnp.cumsum(lengths), jnp.arange(rows * top), side="right").astype(jnp.int32)
    grid = items.reshape(top, rows).T
    grid = grid[jax.random.permutation(jax.random.fold_in(own, 1), rows)]
    rotation = jax.random.randint(jax.random.fold_in(own, 2), (rows, 1), 0, top)
    return jnp.take_along_axis(grid, (jnp.arange(top)[None, :] + rotation) % top, axis=1)


def shares(number_of, total, limit, lean, full):
    weights = [(1 << 20) // math.isqrt(rank ** lean) + 1 for rank in range(1, number_of + 1)]
    largest = limit if full else min(limit, max(-(-total // number_of), total * weights[0] // sum(weights)))
    least = 1 if total - largest >= number_of - 1 else 0
    counts, rest = [largest] + [least] * (number_of - 1), total - largest - least * (number_of - 1)
    while rest > 0:
        candidates = [i for i in range(1, number_of) if counts[i] < largest] or [i for i in range(1, number_of) if counts[i] < limit]
        mass, left = sum([weights[i] for i in candidates]), rest
        for i in candidates:
            addition = min(limit - counts[i], max(1, left * weights[i] // mass), rest)
            counts[i] = counts[i] + addition
            rest = rest - addition
    return np.array(counts)


def bell_draw(stream_key, extent, deviation, reach, cuts=(), held_as=jnp.bfloat16):
    values = deviation * jax.random.normal(stream_key, extent, jnp.float32)
    if cuts:
        values = values * shard_levels(stream_key, extent, cuts, -0.22, 0.18)
    return jnp.clip(values, -reach, reach).astype(held_as)


def setup_inputs(seed: int = 0, part: int = 0) -> dict:
    key_of = jax.random.split(jax.random.key(seed), 10)
    own_keys = jax.random.split(jax.random.fold_in(key_of[9], part), 10)
    tokens = bell_draw(own_keys[0], (TOKENS, D), 1.0, 6.0, ((0, 16),))
    route_ids_keys = jax.random.split(jax.random.fold_in(own_keys[1], 1), TOKENS // TOKENS)
    route_ids_turns = jax.random.permutation(jax.random.fold_in(own_keys[1], 3), TOKENS // TOKENS)
    route_ids = jax.vmap(lambda own, number: deal_out(jax.random.fold_in(own_keys[1], 2), own, number, TOKENS, EXPERTS, TOP, CAP, 2))(route_ids_keys, route_ids_turns).reshape((TOKENS, TOP))
    route_gates = jnp.clip(jax.random.uniform(own_keys[2], (TOKENS, TOP), jnp.float32, 0.2, 1.0), 0.2, 1.0)
    dense_gate = bell_draw(key_of[3], (D, FFD), D ** -0.5, 0.0625, ((1, 16),))
    dense_up = bell_draw(key_of[4], (D, FFD), D ** -0.5, 0.0625, ((1, 16),))
    dense_down = bell_draw(key_of[5], (FFD, D), FFD ** -0.5, 0.078125, ((1, 16),))
    expert_gate = bell_draw(key_of[6], (D, EXP_COLS), D ** -0.5, 0.0625, ((1, 16),))
    expert_up = bell_draw(key_of[7], (D, EXP_COLS), D ** -0.5, 0.0625, ((1, 16),))
    expert_down = bell_draw(key_of[8], (EXP_COLS, D), EH ** -0.5, 0.09375, ((0, 16),))
    return {"tokens": tokens, "route_ids": route_ids, "route_gates": route_gates, "dense_gate": dense_gate, "dense_up": dense_up, "dense_down": dense_down, "expert_gate": expert_gate, "expert_up": expert_up, "expert_down": expert_down}


def swiglu(row_block, w_gate, w_up, w_down):
    gate = jnp.dot(row_block, w_gate, preferred_element_type=jnp.float32)
    upward = jnp.dot(row_block, w_up, preferred_element_type=jnp.float32)
    hidden = (jax.nn.silu(gate) * upward).astype(jnp.bfloat16)
    return jnp.dot(hidden, w_down, preferred_element_type=jnp.float32)


def reference(tokens, route_ids, route_gates, dense_gate, dense_up, dense_down, expert_gate, expert_up, expert_down):
    dense_out = swiglu(tokens, dense_gate, dense_up, dense_down)

    def one_expert(running, expert):
        offset = (expert * EH).astype(jnp.int32)
        w_gate = lax.dynamic_slice_in_dim(expert_gate, offset, EH, 1)
        w_up = lax.dynamic_slice_in_dim(expert_up, offset, EH, 1)
        w_down = lax.dynamic_slice_in_dim(expert_down, offset, EH, 0)
        weight = jnp.sum(jnp.where(route_ids == expert, route_gates, jnp.zeros_like(route_gates)), axis=1)
        return running + weight[:, None] * swiglu(tokens, w_gate, w_up, w_down), None

    moe_out, _ = lax.scan(one_expert, jnp.zeros((TOKENS, D), jnp.float32), jnp.arange(EXPERTS, dtype=jnp.int32))
    return (tokens.astype(jnp.float32) + dense_out + moe_out).astype(jnp.bfloat16)
```

```python
import jax
import jax.numpy as jnp
from jax import lax
from jax.sharding import PartitionSpec as P

EH = 4096


def exchange(value, bit, size):
    return lax.ppermute(value, "gx", [(i, i ^ bit) for i in range(size)])


def gather_xor(rows, size):
    blocks = rows[None]
    bits = []
    bit = size // 2
    while bit:
        bits.append(bit)
        other = exchange(blocks, bit, size)
        blocks = jnp.concatenate([blocks, other], axis=0)
        bit //= 2
    order = [0]
    for taken in bits:
        order = order + [held ^ taken for held in order]
    return blocks, order


def per_device(
    tokens,
    route_ids,
    route_gates,
    dense_gate,
    dense_up,
    dense_down,
    expert_gate,
    expert_up,
    expert_down,
):
    size = lax.axis_size("gx")
    own = lax.axis_index("gx")
    owned, width = tokens.shape
    total = owned * size
    blocks, order = gather_xor(tokens, size)
    rows = blocks.reshape(total, width)
    owners = own ^ jnp.array(order, jnp.int32)
    row_ids = (owners[:, None] * owned + jnp.arange(owned, dtype=jnp.int32)[None, :]).reshape(-1)

    gate = jnp.dot(rows, dense_gate, preferred_element_type=jnp.float32)
    upward = jnp.dot(rows, dense_up, preferred_element_type=jnp.float32)
    dense_hidden = (jax.nn.silu(gate) * upward).astype(jnp.bfloat16)
    place = (row_ids[None, :] == jnp.arange(total, dtype=jnp.int32)[:, None]).astype(jnp.bfloat16)
    dense_hidden = jnp.dot(place, dense_hidden, preferred_element_type=jnp.float32).astype(jnp.bfloat16)
    sent = jnp.broadcast_to(dense_hidden[None], (size,) + dense_hidden.shape)
    hidden_blocks = lax.all_to_all(sent, "gx", split_axis=0, concat_axis=0, tiled=True)

    expert = own * expert_gate.shape[1] // EH
    weights = jnp.sum(jnp.where(route_ids == expert, route_gates, jnp.zeros_like(route_gates)), axis=1)
    weights = jnp.sum(jnp.where(row_ids[:, None] == jnp.arange(total, dtype=jnp.int32)[None, :], weights[None, :], 0.0), axis=1)

    gate = jnp.dot(rows, expert_gate, preferred_element_type=jnp.float32)
    upward = jnp.dot(rows, expert_up, preferred_element_type=jnp.float32)
    hidden = (jax.nn.silu(gate) * upward).astype(jnp.bfloat16)
    partial = weights[:, None] * jnp.dot(hidden, expert_down, preferred_element_type=jnp.float32)

    all_hidden = hidden_blocks.transpose(1, 0, 2).reshape(total, -1)
    dense_part = jnp.dot(all_hidden, dense_down, preferred_element_type=jnp.float32)
    dense_rows = lax.all_to_all(dense_part, "gx", split_axis=0, concat_axis=1, tiled=True)

    partial = partial.reshape(size, owned, width)
    bit = 1
    while bit < size:
        half = partial.shape[0] // 2
        other = exchange(partial[half:].astype(jnp.bfloat16), bit, size)
        partial = partial[:half] + other.astype(jnp.float32)
        bit *= 2
    result = tokens.astype(jnp.float32) + dense_rows + partial[0]
    return result.astype(jnp.bfloat16)


def solution(mesh):
    in_specs = (
        P(("groups", "gx"), None),
        P("groups", None),
        P("groups", None),
        P(None, "gx"),
        P(None, "gx"),
        P(None, "gx"),
        P(None, "gx"),
        P(None, "gx"),
        P("gx", None),
    )
    out_specs = P(("groups", "gx"), None)
    return jax.shard_map(
        per_device, mesh=mesh, in_specs=in_specs, out_specs=out_specs, check_vma=False
    )
```

```python
import functools

import jax
import jax.numpy as jnp
from jax import lax
from jax.experimental import pallas as pl
from jax.experimental.pallas import tpu as pltpu
from jax.sharding import PartitionSpec as P

EH = 4096
CHUNK = 1024
SLOTS = 5
AHEAD = 2
MIB = 1 << 20

VMEM = pl.BlockSpec(memory_space=pltpu.VMEM)
SMEM = pl.BlockSpec(memory_space=pltpu.SMEM)
ANY = pl.BlockSpec(memory_space=pl.ANY)


def in_hbm(x):
    return pltpu.with_memory_space_constraint(x, pltpu.HBM)


def in_vmem(x):
    return pltpu.with_memory_space_constraint(x, pltpu.VMEM)


def cost(flops, moved):
    return pl.CostEstimate(flops=flops, bytes_accessed=moved, transcendentals=0)


def limit(mib):
    return pltpu.CompilerParams(vmem_limit_bytes=mib * MIB)


def dot(x, w):
    return jnp.dot(x, w, preferred_element_type=jnp.float32)


def dot_t(x, w):
    return lax.dot_general(x, w, (((1,), (1,)), ((), ())), preferred_element_type=jnp.float32)


def swiglu_hidden(gate, upward):
    return (jax.nn.silu(gate) * upward).astype(jnp.bfloat16)


def tokens_at(shape, axis, owned):
    p = lax.broadcasted_iota(jnp.int32, shape, axis)
    block, row = p // owned, p % owned
    step = (block & 3) * 4 + ((block >> 2) & 1) * 2 + ((block >> 3) & 1)
    return (lax.axis_index("gx") ^ step) * owned + row


def swap_matrix(rows, owned, to_tokens):
    shape = (rows, rows)
    token = lax.broadcasted_iota(jnp.int32, shape, 0 if to_tokens else 1)
    held = tokens_at(shape, 1 if to_tokens else 0, owned)
    return jnp.where(token == held, 1.0, 0.0).astype(jnp.bfloat16)


def fetch_kernel(ranges, after_ref, *refs):
    count = len(ranges)
    sources, held, done, sems = refs[:count], refs[count : 2 * count], refs[2 * count], refs[2 * count + 1]
    copies = []
    for source, target, (begin, size, pieces) in zip(sources, held, ranges):
        step = size // pieces
        for piece in range(pieces):
            copies.append(
                pltpu.make_async_copy(
                    source.at[pl.ds(begin + piece * step, step)],
                    target.at[pl.ds(piece * step, step)],
                    sems.at[len(copies)],
                )
            )
    for copy in copies:
        copy.start()
    done[0] = 0
    for copy in copies:
        copy.wait()


def fetch(after, *wanted):
    arrays = [w for w, _ in wanted]
    ranges = [r for _, r in wanted]
    *held, done = pl.pallas_call(
        functools.partial(fetch_kernel, ranges),
        out_shape=(
            *[pltpu.VMEM((r[1], w.shape[1]), w.dtype) for w, r in wanted],
            jax.ShapeDtypeStruct((1,), jnp.int32),
        ),
        in_specs=[SMEM] + [ANY] * len(arrays),
        out_specs=(*[VMEM] * len(arrays), SMEM),
        scratch_shapes=[pltpu.SemaphoreType.DMA((sum(r[2] for r in ranges),))],
        cost_estimate=cost(0, sum(2 * r[1] * w.shape[1] for w, r in wanted)),
        compiler_params=limit(1),
    )(after, *[in_hbm(w) for w in arrays])
    return held, done


def join_kernel(count, done_ref, *refs):
    blocks, joined = refs[:count], refs[count]
    at = 0
    for block in blocks:
        size = block.shape[0]
        joined[at : at + size] = block[...]
        at += size


def join(done, *blocks):
    shape = (sum(b.shape[0] for b in blocks),) + blocks[0].shape[1:]
    return pl.pallas_call(
        functools.partial(join_kernel, len(blocks)),
        out_shape=jax.ShapeDtypeStruct(shape, blocks[0].dtype),
        in_specs=[SMEM] + [VMEM] * len(blocks),
        out_specs=VMEM,
        cost_estimate=cost(0, 4 * sum(b.size for b in blocks)),
        compiler_params=limit(4),
    )(done, *blocks)


def dense_in_kernel(owned, mine_ref, other_ref, gate_ref, up_ref, hidden_ref, x):
    half = mine_ref.shape[0]
    x[0:half] = mine_ref[...]
    x[half : 2 * half] = other_ref[...]
    hidden = swiglu_hidden(dot_t(x[...], gate_ref[...]), dot_t(x[...], up_ref[...]))
    hidden_ref[0] = dot(swap_matrix(2 * half, owned, True), hidden).astype(jnp.bfloat16)


def dense_in(owned, mine, other, gate, up):
    rows, width = 2 * mine.shape[0], mine.shape[1]
    return pl.pallas_call(
        functools.partial(dense_in_kernel, owned),
        out_shape=jax.ShapeDtypeStruct((1, rows, gate.shape[0]), jnp.bfloat16),
        in_specs=[VMEM] * 4,
        out_specs=VMEM,
        scratch_shapes=[pltpu.VMEM((rows, width), jnp.bfloat16)],
        cost_estimate=cost(4 * rows * gate.size, 4 * gate.size),
        compiler_params=limit(4),
    )(mine, other, in_vmem(gate), in_vmem(up))


def expert_in_kernel(count, mine_ref, other_ref, *refs):
    gates = refs[:count]
    up_ref, down_ref, hidden_ref, ahead_ref, x, ring, gate_sum, up_sum, sems, ahead_sems = refs[count:]
    half, width = mine_ref.shape
    units = up_ref.shape[1]
    ups = width // CHUNK
    slots = ring.shape[0]

    def up_copy(chunk):
        slot = lax.rem(chunk, slots)
        row = pl.multiple_of(chunk * CHUNK, CHUNK)
        return pltpu.make_async_copy(up_ref.at[pl.ds(row, CHUNK)], ring.at[slot], sems.at[slot])

    def ahead_copy(part):
        row = pl.multiple_of(part * CHUNK, CHUNK)
        return pltpu.make_async_copy(
            down_ref.at[pl.ds(row, CHUNK), pl.ds(0, units)], ahead_ref.at[part], ahead_sems.at[part]
        )

    for chunk in range(slots):
        up_copy(chunk).start()
    x[0:half] = mine_ref[...]
    x[half : 2 * half] = other_ref[...]
    gate_sum[...] = jnp.zeros_like(gate_sum)
    up_sum[...] = jnp.zeros_like(up_sum)

    begin = 0
    for gate_ref in gates:

        @pl.loop(0, gate_ref.shape[0] // CHUNK)
        def _(chunk, gate_ref=gate_ref, begin=begin):
            at = pl.multiple_of(chunk * CHUNK, CHUNK)
            gate_sum[...] += dot(x[:, pl.ds(begin + at, CHUNK)], gate_ref[pl.ds(at, CHUNK), :])

        begin += gate_ref.shape[0]

    @pl.loop(0, ups)
    def _(chunk):
        up_copy(chunk).wait()
        at = pl.ds(pl.multiple_of(chunk * CHUNK, CHUNK), CHUNK)
        up_sum[...] += dot(x[:, at], ring[lax.rem(chunk, slots)])

        @pl.when(chunk + slots < ups)
        def _():
            up_copy(chunk + slots).start()

        @pl.when((chunk + slots >= ups) & (chunk + slots < ups + AHEAD))
        def _():
            ahead_copy(chunk + slots - ups).start()

    hidden_ref[...] = swiglu_hidden(gate_sum[...], up_sum[...])
    for part in range(AHEAD):
        ahead_copy(part).wait()


def expert_in(mine, other, gates, up, down):
    rows, width = 2 * mine.shape[0], mine.shape[1]
    units = up.shape[1]
    return pl.pallas_call(
        functools.partial(expert_in_kernel, len(gates)),
        out_shape=(
            jax.ShapeDtypeStruct((rows, units), jnp.bfloat16),
            pltpu.VMEM((AHEAD, CHUNK, units), jnp.bfloat16),
        ),
        in_specs=[VMEM] * (2 + len(gates)) + [ANY] * 2,
        out_specs=(VMEM, VMEM),
        scratch_shapes=[
            pltpu.VMEM((rows, width), jnp.bfloat16),
            pltpu.VMEM((SLOTS, CHUNK, units), jnp.bfloat16),
            pltpu.VMEM((rows, units), jnp.float32),
            pltpu.VMEM((rows, units), jnp.float32),
            pltpu.SemaphoreType.DMA((SLOTS,)),
            pltpu.SemaphoreType.DMA((AHEAD,)),
        ],
        cost_estimate=cost(4 * rows * up.size, 2 * up.size),
        compiler_params=limit(23),
    )(mine, other, *[in_vmem(g) for g in gates], in_hbm(up), in_hbm(down))


def expert_out_kernel(
    owned, hidden_ref, ids_ref, gates_ref, ahead_ref, down_ref, dense_ref, out_ref, held_ref, ring, sems
):
    rows, units = hidden_ref.shape
    width = out_ref.shape[1]
    blocks = width // units
    copies = []
    for block in range(1, blocks):
        for part in range(2):
            copies.append(
                pltpu.make_async_copy(
                    down_ref.at[pl.ds(part * CHUNK, CHUNK), pl.ds(block * units, units)],
                    ring.at[len(copies)],
                    sems.at[len(copies)],
                )
            )
    last = len(copies)
    for part in range(2):
        copies.append(
            pltpu.make_async_copy(
                down_ref.at[pl.ds(part * CHUNK, CHUNK), pl.ds(blocks * units, CHUNK)],
                ring.at[last, :, pl.ds(part * CHUNK, CHUNK)],
                sems.at[len(copies)],
            )
        )
    copies.append(pltpu.make_async_copy(dense_ref, held_ref, sems.at[len(copies)]))
    for copy in copies:
        copy.start()

    expert = lax.axis_index("gx") * units // EH
    weights = jnp.sum(jnp.where(ids_ref[...] == expert, gates_ref[...], 0.0), axis=0, keepdims=True)
    token = lax.broadcasted_iota(jnp.int32, (rows, rows), 1)
    scale = jnp.sum(jnp.where(token == tokens_at((rows, rows), 0, owned), weights, 0.0), axis=1, keepdims=True)

    first, second = hidden_ref[:, 0:CHUNK], hidden_ref[:, CHUNK : 2 * CHUNK]
    out_ref[:, 0:units] = scale * (dot(first, ahead_ref[0]) + dot(second, ahead_ref[1]))
    for block in range(1, blocks):
        n = 2 * (block - 1)
        copies[n].wait()
        copies[n + 1].wait()
        out_ref[:, block * units : (block + 1) * units] = scale * (dot(first, ring[n]) + dot(second, ring[n + 1]))
    copies[last].wait()
    copies[last + 1].wait()
    out_ref[:, blocks * units :] = scale * (
        dot(first, ring[last, :, 0:CHUNK]) + dot(second, ring[last, :, CHUNK : 2 * CHUNK])
    )
    copies[last + 2].wait()


def expert_out(owned, hidden, ids, gates, ahead, down, dense_down):
    rows, units = hidden.shape
    width = down.shape[1]
    chunks = down.size // (CHUNK * units) - AHEAD
    return pl.pallas_call(
        functools.partial(expert_out_kernel, owned),
        out_shape=(
            jax.ShapeDtypeStruct((rows, width), jnp.float32),
            pltpu.VMEM(dense_down.shape, dense_down.dtype),
        ),
        in_specs=[VMEM] * 4 + [ANY] * 2,
        out_specs=(VMEM, VMEM),
        scratch_shapes=[
            pltpu.VMEM((chunks, CHUNK, units), jnp.bfloat16),
            pltpu.SemaphoreType.DMA((chunks + 2,)),
        ],
        cost_estimate=cost(2 * rows * down.size, 2 * down.size),
        compiler_params=limit(24),
    )(hidden, ids, gates, in_vmem(ahead), in_hbm(down), in_hbm(dense_down))


def dense_out_kernel(owned, part_ref, b0, b1, b2, b3, down_ref, keep_ref, send_ref, held, joined, wide):
    near, rows, units = b0.shape
    half = rows // 2
    columns, width = down_ref.shape[0], part_ref.shape[1]
    own = lax.axis_index("gx")
    for z, blocks in enumerate((b0, b1, b2, b3)):
        held[z * near : (z + 1) * near] = blocks[...]
    for j in range(4 * near):
        joined[:, j * units : (j + 1) * units] = held[own ^ j]
    dense_rows = dot(swap_matrix(rows, owned, False), joined[...]).astype(jnp.bfloat16)
    wide[...] = jnp.zeros_like(wide)
    wide[:, 0:columns] = dot_t(dense_rows, down_ref[...])
    start = own * columns
    base = jnp.minimum(start // 128 * 128, width - wide.shape[1])
    moved = pltpu.roll(wide[...], start - base, 1)
    at = pl.ds(pl.multiple_of(base, 128), wide.shape[1])
    keep_ref[...] = part_ref[0:half]
    send_ref[...] = part_ref[half:].astype(jnp.bfloat16)
    keep_ref[:, at] += moved[:half]
    send_ref[:, at] = (part_ref[half:, at] + moved[half:]).astype(jnp.bfloat16)


def dense_out(owned, part, blocks, down):
    near, rows, units = blocks[0].shape
    columns, inner = down.shape
    width = part.shape[1]
    window = -(-(columns + 64) // 128) * 128 if columns % 64 == 0 else -(-(columns + 127) // 128) * 128
    return pl.pallas_call(
        functools.partial(dense_out_kernel, owned),
        out_shape=(
            jax.ShapeDtypeStruct((rows // 2, width), jnp.float32),
            jax.ShapeDtypeStruct((rows // 2, width), jnp.bfloat16),
        ),
        in_specs=[VMEM] * 6,
        out_specs=(VMEM, VMEM),
        scratch_shapes=[
            pltpu.VMEM((4 * near, rows, units), jnp.bfloat16),
            pltpu.VMEM((rows, inner), jnp.bfloat16),
            pltpu.VMEM((rows, window), jnp.float32),
        ],
        cost_estimate=cost(2 * rows * down.size, 2 * down.size),
        compiler_params=limit(8),
    )(part, *blocks, in_vmem(down))


def four_by_two(
    tokens,
    route_ids,
    route_gates,
    dense_gate,
    dense_up,
    dense_down,
    expert_gate,
    expert_up,
    expert_down,
):
    owned, width = tokens.shape
    dense_gate, dense_up, dense_down = dense_gate.T, dense_up.T, dense_down.T

    def swap(value, step):
        return lax.ppermute(value, "gx", [(i, i ^ step) for i in range(16)])

    none = jnp.zeros((1,), jnp.int32)
    along_z = [swap(tokens, 4 * z) for z in (1, 2, 3)]
    (gate_a,), done = fetch(none, (expert_gate, (0, 3 * CHUNK, 3)))
    mine = join(done, tokens, *along_z)
    along_x = swap(mine, 2)
    (gate_b,), done = fetch(done, (expert_gate, (3 * CHUNK, 3 * CHUNK, 3)))
    mine = join(done, mine, along_x)
    other = swap(mine, 1)
    units = dense_gate.shape[0]
    (gate_c, dense_gate, dense_up), done = fetch(
        done,
        (expert_gate, (6 * CHUNK, width - 6 * CHUNK, 1)),
        (dense_gate, (0, units, 1)),
        (dense_up, (0, units, 1)),
    )

    block = dense_in(owned, mine, other, dense_gate, dense_up)
    block = join(done, block, swap(block, 1))
    along_x = swap(block, 2)
    hidden, ahead = expert_in(mine, other, (gate_a, gate_b, gate_c), expert_up, expert_down)
    block = join(done, block, along_x)
    blocks = [block] + [swap(block, 4 * z) for z in (1, 2, 3)]
    part, dense_down = expert_out(owned, hidden, route_ids.T, route_gates.T, ahead, expert_down, dense_down)
    keep, send = dense_out(owned, part, blocks, dense_down)

    half = keep.shape[0] // 2
    keep = keep + swap(send, 1).astype(jnp.float32)
    keep = keep[:half] + swap(keep[half:].astype(jnp.bfloat16), 2).astype(jnp.float32)
    rest = keep.astype(jnp.bfloat16)
    total = tokens.astype(jnp.float32) + keep[:owned]
    for z in (1, 2, 3):
        total = total + swap(rest[z * owned : (z + 1) * owned], 4 * z).astype(jnp.float32)
    return total.astype(jnp.bfloat16)


def swiglu(row_block, w_gate, w_up, w_down):
    gate = jnp.dot(row_block, w_gate, preferred_element_type=jnp.float32)
    upward = jnp.dot(row_block, w_up, preferred_element_type=jnp.float32)
    hidden = (jax.nn.silu(gate) * upward).astype(jnp.bfloat16)
    return jnp.dot(hidden, w_down, preferred_element_type=jnp.float32)


def any_size(
    tokens,
    route_ids,
    route_gates,
    dense_gate,
    dense_up,
    dense_down,
    expert_gate,
    expert_up,
    expert_down,
):
    gathered = lax.all_gather(tokens, "gx", axis=0, tiled=True)
    total_rows = gathered.shape[0]
    model_width = gathered.shape[1]
    own_index = lax.axis_index("gx")
    gate = jnp.dot(gathered, dense_gate, preferred_element_type=jnp.float32)
    upward = jnp.dot(gathered, dense_up, preferred_element_type=jnp.float32)
    dense_hidden = (jax.nn.silu(gate) * upward).astype(jnp.bfloat16)
    dense_part = jnp.dot(
        lax.all_gather(dense_hidden, "gx", axis=1, tiled=True),
        dense_down,
        preferred_element_type=jnp.float32,
    )
    slice_width = expert_gate.shape[1]
    expert = own_index * slice_width // EH
    flat_ids = route_ids.reshape(-1)
    flat_gates = route_gates.reshape(-1)
    matches = flat_ids == expert
    position = jnp.cumsum(matches.astype(jnp.int32)) - 1
    target = jnp.where(matches, position, total_rows)
    source_row = jnp.arange(flat_ids.shape[0], dtype=jnp.int32) // route_ids.shape[1]
    slot_rows = jnp.zeros((total_rows,), jnp.int32).at[target].set(source_row, mode="drop")
    slot_weights = jnp.zeros((total_rows,), jnp.float32).at[target].set(flat_gates, mode="drop")
    picked = gathered[slot_rows]
    slot_out = swiglu(picked, expert_gate, expert_up, expert_down)
    weighted = slot_weights[:, None] * slot_out
    expert_term = jnp.zeros((total_rows, model_width), jnp.float32).at[slot_rows].add(weighted)
    moe_rows = lax.psum_scatter(expert_term, "gx", scatter_dimension=0, tiled=True)
    dense_rows = lax.all_to_all(dense_part, "gx", split_axis=0, concat_axis=1, tiled=True)
    result = tokens.astype(jnp.float32) + dense_rows + moe_rows
    return result.astype(jnp.bfloat16)


def solution(mesh):
    in_specs = (
        P(("groups", "gx"), None),
        P("groups", None),
        P("groups", None),
        P(None, "gx"),
        P(None, "gx"),
        P(None, "gx"),
        P(None, "gx"),
        P(None, "gx"),
        P("gx", None),
    )
    out_specs = P(("groups", "gx"), None)

    def layer(tokens, *rest):
        size = mesh.shape["gx"]
        width, units = tokens.shape[1], rest[-3].shape[1] // size
        fits = size == 16 and units == 2 * CHUNK and width == 7 * CHUNK
        body = four_by_two if fits else any_size
        whole = jax.shard_map(body, mesh=mesh, in_specs=in_specs, out_specs=out_specs, check_vma=False)
        return whole(tokens, *rest)

    return layer
```

```python
import functools

import jax
import jax.numpy as jnp
from jax import lax
from jax.experimental import pallas as pl
from jax.experimental.pallas import tpu as pltpu
from jax.sharding import PartitionSpec as P

EH = 4096
CHUNK = 1024
PER = 7
SLOTS = 4
AHEAD = (3, 2, 0, 2, 0)
MIB = 1 << 20

VMEM = pl.BlockSpec(memory_space=pltpu.VMEM)
SMEM = pl.BlockSpec(memory_space=pltpu.SMEM)
ANY = pl.BlockSpec(memory_space=pl.ANY)


def in_hbm(x):
    return pltpu.with_memory_space_constraint(x, pltpu.HBM)


def in_vmem(x):
    return pltpu.with_memory_space_constraint(x, pltpu.VMEM)


def cost(flops, moved):
    return pl.CostEstimate(flops=flops, bytes_accessed=moved, transcendentals=0)


def limit(mib):
    return pltpu.CompilerParams(vmem_limit_bytes=mib * MIB)


def dot(x, w):
    return jnp.dot(x, w, preferred_element_type=jnp.float32)


def dot_t(x, w):
    return lax.dot_general(x, w, (((1,), (1,)), ((), ())), preferred_element_type=jnp.float32)


def swiglu_hidden(gate, upward):
    return (jax.nn.silu(gate) * upward).astype(jnp.bfloat16)


def tokens_at(shape, axis, owned):
    p = lax.broadcasted_iota(jnp.int32, shape, axis)
    block, row = p // owned, p % owned
    step = (block & 3) * 4 + ((block >> 2) & 1) * 2 + ((block >> 3) & 1)
    return (lax.axis_index("gx") ^ step) * owned + row


def swap_matrix(rows, owned, to_tokens):
    shape = (rows, rows)
    token = lax.broadcasted_iota(jnp.int32, shape, 0 if to_tokens else 1)
    held = tokens_at(shape, 1 if to_tokens else 0, owned)
    return jnp.where(token == held, 1.0, 0.0).astype(jnp.bfloat16)


def chunk_source(chunk, gate_ref, up_ref):
    source = gate_ref if chunk < PER else up_ref
    return source.at[pl.ds(chunk % PER * CHUNK, CHUNK)]


def start_copies(pairs, sems):
    copies = [pltpu.make_async_copy(source, target, sems.at[n]) for n, (source, target) in enumerate(pairs)]
    for copy in copies:
        copy.start()
    return copies


def wait_copies(copies):
    for copy in copies:
        copy.wait()


def chunk_shapes(count):
    return [pltpu.VMEM((CHUNK, 2 * CHUNK), jnp.bfloat16)] * count


def fetch_kernel(chunks, whole_count, tied, *refs):
    refs = refs[1:] if tied else refs
    gate_ref, up_ref, refs = refs[0], refs[1], refs[2:]
    wholes, refs = refs[:whole_count], refs[whole_count:]
    count = len(chunks)
    held, targets, (done_ref, sems) = refs[:count], refs[count : count + whole_count], refs[count + whole_count :]
    pairs = [(chunk_source(c, gate_ref, up_ref), ref) for c, ref in zip(chunks, held)]
    copies = start_copies(pairs + list(zip(wholes, targets)), sems)
    done_ref[...] = jnp.zeros_like(done_ref)
    wait_copies(copies)


def fetch(after, chunks, gate, up, *wholes):
    tied = after is not None
    count = len(chunks)
    found = pl.pallas_call(
        functools.partial(fetch_kernel, chunks, len(wholes), tied),
        out_shape=(
            *chunk_shapes(count),
            *[pltpu.VMEM(w.shape, w.dtype) for w in wholes],
            pltpu.VMEM((8, 128), jnp.float32),
        ),
        in_specs=[VMEM] * tied + [ANY] * (2 + len(wholes)),
        out_specs=(VMEM,) * (count + len(wholes) + 1),
        scratch_shapes=[pltpu.SemaphoreType.DMA((count + len(wholes),))],
        cost_estimate=cost(0, 4 * count * CHUNK * CHUNK + sum(2 * w.size for w in wholes)),
        compiler_params=limit(1),
    )(*([in_vmem(after)] if tied else []), in_hbm(gate), in_hbm(up), *[in_hbm(w) for w in wholes])
    return list(found[:count]), *found[count:]


def join_kernel(count, *refs):
    blocks, joined = refs[-1 - count : -1], refs[-1]
    at = 0
    for block in blocks:
        size = block.shape[0]
        joined[at : at + size] = block[...]
        at += size


def join(done, *blocks):
    shape = (sum(b.shape[0] for b in blocks),) + blocks[0].shape[1:]
    ties = [] if done is None else [in_vmem(done)]
    return pl.pallas_call(
        functools.partial(join_kernel, len(blocks)),
        out_shape=pltpu.VMEM(shape, blocks[0].dtype),
        in_specs=[VMEM] * (len(ties) + len(blocks)),
        out_specs=VMEM,
        cost_estimate=cost(0, 4 * sum(b.size for b in blocks)),
        compiler_params=limit(4),
    )(*ties, *blocks)


def dense_in_kernel(
    owned, chunks, mine_ref, other_ref, dense_gate, dense_up, gate_ref, up_ref, hidden_ref, x_ref, *refs
):
    held, sems = refs[:-1], refs[-1]
    copies = start_copies([(chunk_source(c, gate_ref, up_ref), ref) for c, ref in zip(chunks, held)], sems)
    half = mine_ref.shape[0]
    x_ref[0:half] = mine_ref[...]
    x_ref[half : 2 * half] = other_ref[...]
    hidden = swiglu_hidden(dot_t(x_ref[...], dense_gate[...]), dot_t(x_ref[...], dense_up[...]))
    hidden_ref[0] = dot(swap_matrix(2 * half, owned, True), hidden).astype(jnp.bfloat16)
    wait_copies(copies)


def dense_in(owned, chunks, mine, other, dense_gate, dense_up, gate, up):
    rows, width = 2 * mine.shape[0], mine.shape[1]
    count = len(chunks)
    hidden, x, *held = pl.pallas_call(
        functools.partial(dense_in_kernel, owned, chunks),
        out_shape=(
            pltpu.VMEM((1, rows, dense_gate.shape[0]), jnp.bfloat16),
            pltpu.VMEM((rows, width), jnp.bfloat16),
            *chunk_shapes(count),
        ),
        in_specs=[VMEM] * 4 + [ANY] * 2,
        out_specs=(VMEM,) * (2 + count),
        scratch_shapes=[pltpu.SemaphoreType.DMA((max(count, 1),))],
        cost_estimate=cost(4 * rows * dense_gate.size, 4 * dense_gate.size),
        compiler_params=limit(4),
    )(in_vmem(mine), other, in_vmem(dense_gate), in_vmem(dense_up), in_hbm(gate), in_hbm(up))
    return hidden, x, held


def expert_kernel(owned, there, x_ref, ids_ref, gates_ref, *refs):
    ready, refs = refs[:there], refs[there:]
    gate_ref, up_ref, down_ref, dense_ref, out_ref, dense_held, gate_sum, up_sum, hidden, ring, sems = refs
    rows, units = gate_sum.shape
    slots = ring.shape[0]
    blocks = PER // 2
    pieces = [[(chunk_source(c, gate_ref, up_ref), 0)] for c in range(there, 2 * PER)]
    streamed = len(pieces)
    for block in range(blocks):
        for part in range(2):
            held = down_ref.at[pl.ds(part * CHUNK, CHUNK), pl.ds(block * units, units)]
            pieces.append([(held, 0)])
    parts = [down_ref.at[pl.ds(part * CHUNK, CHUNK), pl.ds(blocks * units, CHUNK)] for part in range(2)]
    pieces.append([(parts[0], 0), (parts[1], CHUNK)])
    total = len(pieces)
    found = {}
    dense_copy = pltpu.make_async_copy(dense_ref, dense_held, sems.at[slots + 1])

    def issue(n):
        if n < total:
            found[n] = []
            for source, column in pieces[n]:
                slot = ring.at[n % slots]
                target = slot if len(pieces[n]) == 1 else slot.at[:, pl.ds(column, CHUNK)]
                copy = pltpu.make_async_copy(source, target, sems.at[slots if column else n % slots])
                copy.start()
                found[n].append(copy)
        elif n == total:
            dense_copy.start()

    def arrived(n):
        wait_copies(found[n])
        return ring.at[n % slots]

    for n in range(slots):
        issue(n)

    begun = set()

    def add(chunk, weights):
        target = gate_sum if chunk < PER else up_sum
        at = chunk % PER * CHUNK
        product = dot(x_ref[:, at : at + CHUNK], weights[...])
        target[...] = target[...] + product if chunk // PER in begun else product
        begun.add(chunk // PER)

    lead = max(there - streamed, 1)
    for n in range(lead):
        add(n, ready[n])
    for n in range(max(there - lead, streamed)):
        if n < streamed:
            add(there + n, arrived(n))
            issue(n + slots)
        if lead + n < there:
            add(lead + n, ready[lead + n])
    hidden[...] = swiglu_hidden(gate_sum[...], up_sum[...])

    expert = lax.axis_index("gx") * units // EH
    weights = jnp.sum(jnp.where(ids_ref[...] == expert, gates_ref[...], 0.0), axis=0, keepdims=True)
    token = lax.broadcasted_iota(jnp.int32, (rows, rows), 1)
    scale = jnp.sum(jnp.where(token == tokens_at((rows, rows), 0, owned), weights, 0.0), axis=1, keepdims=True)

    first, second = hidden[:, 0:CHUNK], hidden[:, CHUNK : 2 * CHUNK]
    for block in range(blocks):
        n = streamed + 2 * block
        at = pl.ds(block * units, units)
        out_ref[:, at] = dot(first, arrived(n)[...])
        issue(n + slots)
        out_ref[:, at] = scale * (out_ref[:, at] + dot(second, arrived(n + 1)[...]))
        issue(n + 1 + slots)
    last = arrived(total - 1)
    both = dot(first, last[:, 0:CHUNK]) + dot(second, last[:, CHUNK : 2 * CHUNK])
    out_ref[:, blocks * units :] = scale * both
    dense_copy.wait()


def expert_block(owned, x, ids, gates, ready, gate, up, down, dense_down):
    rows, width = x.shape
    units = gate.shape[1]
    return pl.pallas_call(
        functools.partial(expert_kernel, owned, len(ready)),
        out_shape=(
            pltpu.VMEM((rows, width), jnp.float32),
            pltpu.VMEM(dense_down.shape, dense_down.dtype),
        ),
        in_specs=[VMEM] * (3 + len(ready)) + [ANY] * 4,
        out_specs=(VMEM, VMEM),
        scratch_shapes=[
            pltpu.VMEM((rows, units), jnp.float32),
            pltpu.VMEM((rows, units), jnp.float32),
            pltpu.VMEM((rows, units), jnp.bfloat16),
            pltpu.VMEM((SLOTS, CHUNK, units), jnp.bfloat16),
            pltpu.SemaphoreType.DMA((SLOTS + 2,)),
        ],
        cost_estimate=cost(6 * rows * down.size, 4 * down.size),
        compiler_params=limit(4 * SLOTS + 3),
    )(
        in_vmem(x), ids, gates, *[in_vmem(r) for r in ready],
        in_hbm(gate), in_hbm(up), in_hbm(down), in_hbm(dense_down),
    )


def dense_out_kernel(owned, part_ref, b0, b1, b2, b3, down_ref, keep_ref, send_ref, held, joined, wide):
    near, rows, units = b0.shape
    half = rows // 2
    columns, width = down_ref.shape[0], part_ref.shape[1]
    own = lax.axis_index("gx")
    for z, blocks in enumerate((b0, b1, b2, b3)):
        held[z * near : (z + 1) * near] = blocks[...]
    for j in range(4 * near):
        joined[:, j * units : (j + 1) * units] = held[own ^ j]
    dense_rows = dot(swap_matrix(rows, owned, False), joined[...]).astype(jnp.bfloat16)
    wide[...] = jnp.zeros_like(wide)
    wide[:, 0:columns] = dot_t(dense_rows, down_ref[...])
    start = own * columns
    base = jnp.minimum(start // 128 * 128, width - wide.shape[1])
    moved = pltpu.roll(wide[...], start - base, 1)
    at = pl.ds(pl.multiple_of(base, 128), wide.shape[1])
    keep_ref[...] = part_ref[0:half]
    send_ref[...] = part_ref[half:].astype(jnp.bfloat16)
    keep_ref[:, at] += moved[:half]
    send_ref[:, at] = (part_ref[half:, at] + moved[half:]).astype(jnp.bfloat16)


def dense_out(owned, part, blocks, down):
    near, rows, units = blocks[0].shape
    columns, inner = down.shape
    width = part.shape[1]
    window = -(-(columns + 64) // 128) * 128 if columns % 64 == 0 else -(-(columns + 127) // 128) * 128
    return pl.pallas_call(
        functools.partial(dense_out_kernel, owned),
        out_shape=(
            jax.ShapeDtypeStruct((rows // 2, width), jnp.float32),
            jax.ShapeDtypeStruct((rows // 2, width), jnp.bfloat16),
        ),
        in_specs=[VMEM] * 6,
        out_specs=(VMEM, VMEM),
        scratch_shapes=[
            pltpu.VMEM((4 * near, rows, units), jnp.bfloat16),
            pltpu.VMEM((rows, inner), jnp.bfloat16),
            pltpu.VMEM((rows, window), jnp.float32),
        ],
        cost_estimate=cost(2 * rows * down.size, 2 * down.size),
        compiler_params=limit(8),
    )(in_vmem(part), *blocks, in_vmem(down))


def four_by_two(
    tokens,
    route_ids,
    route_gates,
    dense_gate,
    dense_up,
    dense_down,
    expert_gate,
    expert_up,
    expert_down,
):
    owned, width = tokens.shape
    dense_gate, dense_up, dense_down = dense_gate.T, dense_up.T, dense_down.T

    def swap(value, step):
        return lax.ppermute(value, "gx", [(i, i ^ step) for i in range(16)])

    ends = [sum(AHEAD[: n + 1]) for n in range(len(AHEAD))]
    chunks = [range(end - count, end) for count, end in zip(AHEAD, ends)]
    streams = (expert_gate, expert_up)
    along_z = [swap(tokens, 4 * z) for z in (1, 2, 3)]
    ready, done = fetch(None, chunks[0], *streams)
    mine = join(done, tokens, *along_z)
    along_x = swap(mine, 2)
    more, done = fetch(done, chunks[1], *streams)
    ready += more
    mine = join(done, mine, along_x)
    other = swap(mine, 1)
    more, dense_gate, dense_up, _ = fetch(done, chunks[2], *streams, dense_gate, dense_up)
    ready += more

    block, x, more = dense_in(owned, chunks[3], mine, other, dense_gate, dense_up, *streams)
    ready += more
    block = join(None, block, swap(block, 1))
    along_x = swap(block, 2)
    if AHEAD[4]:
        more, done = fetch(done, chunks[4], *streams)
        ready += more
        block = join(done, block, along_x)
    else:
        block = join(None, block, along_x)
    blocks = [block] + [swap(block, 4 * z) for z in (1, 2, 3)]
    part, dense_down = expert_block(
        owned, x, route_ids.T, route_gates.T, ready, expert_gate, expert_up, expert_down, dense_down
    )
    keep, send = dense_out(owned, part, blocks, dense_down)

    half = keep.shape[0] // 2
    keep = keep + swap(send, 1).astype(jnp.float32)
    keep = keep[:half] + swap(keep[half:].astype(jnp.bfloat16), 2).astype(jnp.float32)
    rest = keep.astype(jnp.bfloat16)
    total = tokens.astype(jnp.float32) + keep[:owned]
    for z in (1, 2, 3):
        total = total + swap(rest[z * owned : (z + 1) * owned], 4 * z).astype(jnp.float32)
    return total.astype(jnp.bfloat16)


def swiglu(row_block, w_gate, w_up, w_down):
    gate = jnp.dot(row_block, w_gate, preferred_element_type=jnp.float32)
    upward = jnp.dot(row_block, w_up, preferred_element_type=jnp.float32)
    hidden = (jax.nn.silu(gate) * upward).astype(jnp.bfloat16)
    return jnp.dot(hidden, w_down, preferred_element_type=jnp.float32)


def any_size(
    tokens,
    route_ids,
    route_gates,
    dense_gate,
    dense_up,
    dense_down,
    expert_gate,
    expert_up,
    expert_down,
):
    gathered = lax.all_gather(tokens, "gx", axis=0, tiled=True)
    total_rows = gathered.shape[0]
    model_width = gathered.shape[1]
    own_index = lax.axis_index("gx")
    gate = jnp.dot(gathered, dense_gate, preferred_element_type=jnp.float32)
    upward = jnp.dot(gathered, dense_up, preferred_element_type=jnp.float32)
    dense_hidden = (jax.nn.silu(gate) * upward).astype(jnp.bfloat16)
    dense_part = jnp.dot(
        lax.all_gather(dense_hidden, "gx", axis=1, tiled=True),
        dense_down,
        preferred_element_type=jnp.float32,
    )
    slice_width = expert_gate.shape[1]
    expert = own_index * slice_width // EH
    flat_ids = route_ids.reshape(-1)
    flat_gates = route_gates.reshape(-1)
    matches = flat_ids == expert
    position = jnp.cumsum(matches.astype(jnp.int32)) - 1
    target = jnp.where(matches, position, total_rows)
    source_row = jnp.arange(flat_ids.shape[0], dtype=jnp.int32) // route_ids.shape[1]
    slot_rows = jnp.zeros((total_rows,), jnp.int32).at[target].set(source_row, mode="drop")
    slot_weights = jnp.zeros((total_rows,), jnp.float32).at[target].set(flat_gates, mode="drop")
    picked = gathered[slot_rows]
    slot_out = swiglu(picked, expert_gate, expert_up, expert_down)
    weighted = slot_weights[:, None] * slot_out
    expert_term = jnp.zeros((total_rows, model_width), jnp.float32).at[slot_rows].add(weighted)
    moe_rows = lax.psum_scatter(expert_term, "gx", scatter_dimension=0, tiled=True)
    dense_rows = lax.all_to_all(dense_part, "gx", split_axis=0, concat_axis=1, tiled=True)
    result = tokens.astype(jnp.float32) + dense_rows + moe_rows
    return result.astype(jnp.bfloat16)


def solution(mesh):
    in_specs = (
        P(("groups", "gx"), None),
        P("groups", None),
        P("groups", None),
        P(None, "gx"),
        P(None, "gx"),
        P(None, "gx"),
        P(None, "gx"),
        P(None, "gx"),
        P("gx", None),
    )
    out_specs = P(("groups", "gx"), None)

    def layer(tokens, *rest):
        size = mesh.shape["gx"]
        width, units = tokens.shape[1], rest[-3].shape[1] // size
        fits = size == 16 and units == 2 * CHUNK and width == PER * CHUNK
        body = four_by_two if fits else any_size
        whole = jax.shard_map(body, mesh=mesh, in_specs=in_specs, out_specs=out_specs, check_vma=False)
        return whole(tokens, *rest)

    return layer
```

```python
import functools

import jax
import jax.numpy as jnp
from jax import lax
from jax.experimental import pallas as pl
from jax.experimental.pallas import tpu as pltpu
from jax.sharding import PartitionSpec as P

EH = 4096
CHUNK = 1024
PER = 7
SLOTS = 4
AHEAD = (3, 1, 0, 1, 2)
MIB = 1 << 20

VMEM = pl.BlockSpec(memory_space=pltpu.VMEM)
SMEM = pl.BlockSpec(memory_space=pltpu.SMEM)
ANY = pl.BlockSpec(memory_space=pl.ANY)


def in_hbm(x):
    return pltpu.with_memory_space_constraint(x, pltpu.HBM)


def in_vmem(x):
    return pltpu.with_memory_space_constraint(x, pltpu.VMEM)


def cost(flops, moved):
    return pl.CostEstimate(flops=flops, bytes_accessed=moved, transcendentals=0)


def limit(mib):
    return pltpu.CompilerParams(vmem_limit_bytes=mib * MIB)


def dot(x, w):
    return jnp.dot(x, w, preferred_element_type=jnp.float32)


def dot_t(x, w):
    return lax.dot_general(x, w, (((1,), (1,)), ((), ())), preferred_element_type=jnp.float32)


def swiglu_hidden(gate, upward):
    return (jax.nn.silu(gate) * upward).astype(jnp.bfloat16)


def tokens_at(shape, axis, owned):
    p = lax.broadcasted_iota(jnp.int32, shape, axis)
    block, row = p // owned, p % owned
    step = (block & 3) * 4 + ((block >> 2) & 1) * 2 + ((block >> 3) & 1)
    return (lax.axis_index("gx") ^ step) * owned + row


def swap_matrix(rows, owned, to_tokens):
    shape = (rows, rows)
    token = lax.broadcasted_iota(jnp.int32, shape, 0 if to_tokens else 1)
    held = tokens_at(shape, 1 if to_tokens else 0, owned)
    return jnp.where(token == held, 1.0, 0.0).astype(jnp.bfloat16)


def chunk_source(chunk, gate_ref, up_ref):
    source = gate_ref if chunk < PER else up_ref
    return source.at[pl.ds(chunk % PER * CHUNK, CHUNK)]


def start_copies(pairs, sems):
    copies = [pltpu.make_async_copy(source, target, sems.at[n]) for n, (source, target) in enumerate(pairs)]
    for copy in copies:
        copy.start()
    return copies


def wait_copies(copies):
    for copy in copies:
        copy.wait()


def chunk_shapes(count):
    return [pltpu.VMEM((CHUNK, 2 * CHUNK), jnp.bfloat16)] * count


def fetch_kernel(chunks, whole_count, tied, *refs):
    refs = refs[1:] if tied else refs
    gate_ref, up_ref, refs = refs[0], refs[1], refs[2:]
    wholes, refs = refs[:whole_count], refs[whole_count:]
    count = len(chunks)
    held, targets, (done_ref, sems) = refs[:count], refs[count : count + whole_count], refs[count + whole_count :]
    pairs = [(chunk_source(c, gate_ref, up_ref), ref) for c, ref in zip(chunks, held)]
    copies = start_copies(pairs + list(zip(wholes, targets)), sems)
    done_ref[...] = jnp.zeros_like(done_ref)
    wait_copies(copies)


def fetch(after, chunks, gate, up, *wholes):
    tied = after is not None
    count = len(chunks)
    found = pl.pallas_call(
        functools.partial(fetch_kernel, chunks, len(wholes), tied),
        out_shape=(
            *chunk_shapes(count),
            *[pltpu.VMEM(w.shape, w.dtype) for w in wholes],
            pltpu.VMEM((8, 128), jnp.float32),
        ),
        in_specs=[VMEM] * tied + [ANY] * (2 + len(wholes)),
        out_specs=(VMEM,) * (count + len(wholes) + 1),
        scratch_shapes=[pltpu.SemaphoreType.DMA((count + len(wholes),))],
        cost_estimate=cost(0, 4 * count * CHUNK * CHUNK + sum(2 * w.size for w in wholes)),
        compiler_params=limit(1),
    )(*([in_vmem(after)] if tied else []), in_hbm(gate), in_hbm(up), *[in_hbm(w) for w in wholes])
    return list(found[:count]), *found[count:]


def join_kernel(count, *refs):
    blocks, joined = refs[-1 - count : -1], refs[-1]
    at = 0
    for block in blocks:
        size = block.shape[0]
        joined[at : at + size] = block[...]
        at += size


def join(done, *blocks):
    shape = (sum(b.shape[0] for b in blocks),) + blocks[0].shape[1:]
    ties = [] if done is None else [in_vmem(done)]
    return pl.pallas_call(
        functools.partial(join_kernel, len(blocks)),
        out_shape=pltpu.VMEM(shape, blocks[0].dtype),
        in_specs=[VMEM] * (len(ties) + len(blocks)),
        out_specs=VMEM,
        cost_estimate=cost(0, 4 * sum(b.size for b in blocks)),
        compiler_params=limit(4),
    )(*ties, *blocks)


def dense_in_kernel(
    owned, chunks, mine_ref, other_ref, dense_gate, dense_up, gate_ref, up_ref, hidden_ref, x_ref, *refs
):
    held, sems = refs[:-1], refs[-1]
    copies = start_copies([(chunk_source(c, gate_ref, up_ref), ref) for c, ref in zip(chunks, held)], sems)
    half = mine_ref.shape[0]
    x_ref[0:half] = mine_ref[...]
    x_ref[half : 2 * half] = other_ref[...]
    hidden = swiglu_hidden(dot_t(x_ref[...], dense_gate[...]), dot_t(x_ref[...], dense_up[...]))
    hidden_ref[0] = dot(swap_matrix(2 * half, owned, True), hidden).astype(jnp.bfloat16)
    wait_copies(copies)


def dense_in(owned, chunks, mine, other, dense_gate, dense_up, gate, up):
    rows, width = 2 * mine.shape[0], mine.shape[1]
    count = len(chunks)
    hidden, x, *held = pl.pallas_call(
        functools.partial(dense_in_kernel, owned, chunks),
        out_shape=(
            pltpu.VMEM((1, rows, dense_gate.shape[0]), jnp.bfloat16),
            pltpu.VMEM((rows, width), jnp.bfloat16),
            *chunk_shapes(count),
        ),
        in_specs=[VMEM] * 4 + [ANY] * 2,
        out_specs=(VMEM,) * (2 + count),
        scratch_shapes=[pltpu.SemaphoreType.DMA((max(count, 1),))],
        cost_estimate=cost(4 * rows * dense_gate.size, 4 * dense_gate.size),
        compiler_params=limit(4),
    )(in_vmem(mine), other, in_vmem(dense_gate), in_vmem(dense_up), in_hbm(gate), in_hbm(up))
    return hidden, x, held


def expert_kernel(owned, there, x_ref, ids_ref, gates_ref, *refs):
    ready, refs = refs[:there], refs[there:]
    gate_ref, up_ref, down_ref, dense_ref, out_ref, dense_held, gate_sum, up_sum, hidden, ring, sems = refs
    rows, units = gate_sum.shape
    slots = ring.shape[0]
    blocks = PER // 2
    pieces = [[(chunk_source(c, gate_ref, up_ref), 0)] for c in range(there, 2 * PER)]
    streamed = len(pieces)
    for block in range(blocks):
        for part in range(2):
            held = down_ref.at[pl.ds(part * CHUNK, CHUNK), pl.ds(block * units, units)]
            pieces.append([(held, 0)])
    parts = [down_ref.at[pl.ds(part * CHUNK, CHUNK), pl.ds(blocks * units, CHUNK)] for part in range(2)]
    pieces.append([(parts[0], 0), (parts[1], CHUNK)])
    total = len(pieces)
    found = {}
    dense_copy = pltpu.make_async_copy(dense_ref, dense_held, sems.at[slots + 1])

    def issue(n):
        if n < total:
            found[n] = []
            for source, column in pieces[n]:
                slot = ring.at[n % slots]
                target = slot if len(pieces[n]) == 1 else slot.at[:, pl.ds(column, CHUNK)]
                copy = pltpu.make_async_copy(source, target, sems.at[slots if column else n % slots])
                copy.start()
                found[n].append(copy)
        elif n == total:
            dense_copy.start()

    def arrived(n):
        wait_copies(found[n])
        return ring.at[n % slots]

    for n in range(slots):
        issue(n)

    begun = set()

    def add(chunk, weights):
        target = gate_sum if chunk < PER else up_sum
        at = chunk % PER * CHUNK
        product = dot(x_ref[:, at : at + CHUNK], weights[...])
        target[...] = target[...] + product if chunk // PER in begun else product
        begun.add(chunk // PER)

    lead = max(there - streamed, 1)
    for n in range(lead):
        add(n, ready[n])
    for n in range(max(there - lead, streamed)):
        if n < streamed:
            add(there + n, arrived(n))
            issue(n + slots)
        if lead + n < there:
            add(lead + n, ready[lead + n])
    hidden[...] = swiglu_hidden(gate_sum[...], up_sum[...])

    expert = lax.axis_index("gx") * units // EH
    weights = jnp.sum(jnp.where(ids_ref[...] == expert, gates_ref[...], 0.0), axis=0, keepdims=True)
    token = lax.broadcasted_iota(jnp.int32, (rows, rows), 1)
    scale = jnp.sum(jnp.where(token == tokens_at((rows, rows), 0, owned), weights, 0.0), axis=1, keepdims=True)

    first, second = hidden[:, 0:CHUNK], hidden[:, CHUNK : 2 * CHUNK]
    for block in range(blocks):
        n = streamed + 2 * block
        at = pl.ds(block * units, units)
        out_ref[:, at] = dot(first, arrived(n)[...])
        issue(n + slots)
        out_ref[:, at] = scale * (out_ref[:, at] + dot(second, arrived(n + 1)[...]))
        issue(n + 1 + slots)
    last = arrived(total - 1)
    both = dot(first, last[:, 0:CHUNK]) + dot(second, last[:, CHUNK : 2 * CHUNK])
    out_ref[:, blocks * units :] = scale * both
    dense_copy.wait()


def expert_block(owned, x, ids, gates, ready, gate, up, down, dense_down):
    rows, width = x.shape
    units = gate.shape[1]
    return pl.pallas_call(
        functools.partial(expert_kernel, owned, len(ready)),
        out_shape=(
            pltpu.VMEM((rows, width), jnp.float32),
            pltpu.VMEM(dense_down.shape, dense_down.dtype),
        ),
        in_specs=[VMEM] * (3 + len(ready)) + [ANY] * 4,
        out_specs=(VMEM, VMEM),
        scratch_shapes=[
            pltpu.VMEM((rows, units), jnp.float32),
            pltpu.VMEM((rows, units), jnp.float32),
            pltpu.VMEM((rows, units), jnp.bfloat16),
            pltpu.VMEM((SLOTS, CHUNK, units), jnp.bfloat16),
            pltpu.SemaphoreType.DMA((SLOTS + 2,)),
        ],
        cost_estimate=cost(6 * rows * down.size, 4 * down.size),
        compiler_params=limit(4 * SLOTS + 3),
    )(
        in_vmem(x), ids, gates, *[in_vmem(r) for r in ready],
        in_hbm(gate), in_hbm(up), in_hbm(down), in_hbm(dense_down),
    )


def dense_out_kernel(owned, part_ref, b0, b1, b2, b3, down_ref, keep_ref, send_ref, held, joined, wide):
    near, rows, units = b0.shape
    half = rows // 2
    columns, width = down_ref.shape[0], part_ref.shape[1]
    own = lax.axis_index("gx")
    for z, blocks in enumerate((b0, b1, b2, b3)):
        held[z * near : (z + 1) * near] = blocks[...]
    for j in range(4 * near):
        joined[:, j * units : (j + 1) * units] = held[own ^ j]
    dense_rows = dot(swap_matrix(rows, owned, False), joined[...]).astype(jnp.bfloat16)
    wide[...] = jnp.zeros_like(wide)
    wide[:, 0:columns] = dot_t(dense_rows, down_ref[...])
    start = own * columns
    base = jnp.minimum(start // 128 * 128, width - wide.shape[1])
    moved = pltpu.roll(wide[...], start - base, 1)
    at = pl.ds(pl.multiple_of(base, 128), wide.shape[1])
    keep_ref[...] = part_ref[0:half]
    send_ref[...] = part_ref[half:].astype(jnp.bfloat16)
    keep_ref[:, at] += moved[:half]
    send_ref[:, at] = (part_ref[half:, at] + moved[half:]).astype(jnp.bfloat16)


def dense_out(owned, part, blocks, down):
    near, rows, units = blocks[0].shape
    columns, inner = down.shape
    width = part.shape[1]
    window = -(-(columns + 64) // 128) * 128 if columns % 64 == 0 else -(-(columns + 127) // 128) * 128
    return pl.pallas_call(
        functools.partial(dense_out_kernel, owned),
        out_shape=(
            jax.ShapeDtypeStruct((rows // 2, width), jnp.float32),
            jax.ShapeDtypeStruct((rows // 2, width), jnp.bfloat16),
        ),
        in_specs=[VMEM] * 6,
        out_specs=(VMEM, VMEM),
        scratch_shapes=[
            pltpu.VMEM((4 * near, rows, units), jnp.bfloat16),
            pltpu.VMEM((rows, inner), jnp.bfloat16),
            pltpu.VMEM((rows, window), jnp.float32),
        ],
        cost_estimate=cost(2 * rows * down.size, 2 * down.size),
        compiler_params=limit(8),
    )(in_vmem(part), *blocks, in_vmem(down))


def four_by_two(
    tokens,
    route_ids,
    route_gates,
    dense_gate,
    dense_up,
    dense_down,
    expert_gate,
    expert_up,
    expert_down,
):
    owned, width = tokens.shape
    dense_gate, dense_up, dense_down = dense_gate.T, dense_up.T, dense_down.T

    def swap(value, step):
        return lax.ppermute(value, "gx", [(i, i ^ step) for i in range(16)])

    ends = [sum(AHEAD[: n + 1]) for n in range(len(AHEAD))]
    chunks = [range(end - count, end) for count, end in zip(AHEAD, ends)]
    streams = (expert_gate, expert_up)
    along_z = [swap(tokens, 4 * z) for z in (1, 2, 3)]
    ready, dense_gate, done = fetch(None, chunks[0], *streams, dense_gate)
    mine = join(done, tokens, *along_z)
    along_x = swap(mine, 2)
    more, dense_up, done = fetch(done, chunks[1], *streams, dense_up)
    ready += more
    mine = join(done, mine, along_x)
    other = swap(mine, 1)
    if AHEAD[2]:
        more, _ = fetch(done, chunks[2], *streams)
        ready += more

    block, x, more = dense_in(owned, chunks[3], mine, other, dense_gate, dense_up, *streams)
    ready += more
    near = [block] + [swap(block, step) for step in (1, 2, 3)]
    if AHEAD[4]:
        more, done = fetch(block, chunks[4], *streams)
        ready += more
    else:
        done = None
    block = join(done, *near)
    blocks = [block] + [swap(block, 4 * z) for z in (1, 2, 3)]
    part, dense_down = expert_block(
        owned, x, route_ids.T, route_gates.T, ready, expert_gate, expert_up, expert_down, dense_down
    )
    keep, send = dense_out(owned, part, blocks, dense_down)

    half = keep.shape[0] // 2
    keep = keep + swap(send, 1).astype(jnp.float32)
    keep = keep[:half] + swap(keep[half:].astype(jnp.bfloat16), 2).astype(jnp.float32)
    rest = keep.astype(jnp.bfloat16)
    total = tokens.astype(jnp.float32) + keep[:owned]
    for z in (1, 2, 3):
        total = total + swap(rest[z * owned : (z + 1) * owned], 4 * z).astype(jnp.float32)
    return total.astype(jnp.bfloat16)


def swiglu(row_block, w_gate, w_up, w_down):
    gate = jnp.dot(row_block, w_gate, preferred_element_type=jnp.float32)
    upward = jnp.dot(row_block, w_up, preferred_element_type=jnp.float32)
    hidden = (jax.nn.silu(gate) * upward).astype(jnp.bfloat16)
    return jnp.dot(hidden, w_down, preferred_element_type=jnp.float32)


def any_size(
    tokens,
    route_ids,
    route_gates,
    dense_gate,
    dense_up,
    dense_down,
    expert_gate,
    expert_up,
    expert_down,
):
    gathered = lax.all_gather(tokens, "gx", axis=0, tiled=True)
    total_rows = gathered.shape[0]
    model_width = gathered.shape[1]
    own_index = lax.axis_index("gx")
    gate = jnp.dot(gathered, dense_gate, preferred_element_type=jnp.float32)
    upward = jnp.dot(gathered, dense_up, preferred_element_type=jnp.float32)
    dense_hidden = (jax.nn.silu(gate) * upward).astype(jnp.bfloat16)
    dense_part = jnp.dot(
        lax.all_gather(dense_hidden, "gx", axis=1, tiled=True),
        dense_down,
        preferred_element_type=jnp.float32,
    )
    slice_width = expert_gate.shape[1]
    expert = own_index * slice_width // EH
    flat_ids = route_ids.reshape(-1)
    flat_gates = route_gates.reshape(-1)
    matches = flat_ids == expert
    position = jnp.cumsum(matches.astype(jnp.int32)) - 1
    target = jnp.where(matches, position, total_rows)
    source_row = jnp.arange(flat_ids.shape[0], dtype=jnp.int32) // route_ids.shape[1]
    slot_rows = jnp.zeros((total_rows,), jnp.int32).at[target].set(source_row, mode="drop")
    slot_weights = jnp.zeros((total_rows,), jnp.float32).at[target].set(flat_gates, mode="drop")
    picked = gathered[slot_rows]
    slot_out = swiglu(picked, expert_gate, expert_up, expert_down)
    weighted = slot_weights[:, None] * slot_out
    expert_term = jnp.zeros((total_rows, model_width), jnp.float32).at[slot_rows].add(weighted)
    moe_rows = lax.psum_scatter(expert_term, "gx", scatter_dimension=0, tiled=True)
    dense_rows = lax.all_to_all(dense_part, "gx", split_axis=0, concat_axis=1, tiled=True)
    result = tokens.astype(jnp.float32) + dense_rows + moe_rows
    return result.astype(jnp.bfloat16)


def solution(mesh):
    in_specs = (
        P(("groups", "gx"), None),
        P("groups", None),
        P("groups", None),
        P(None, "gx"),
        P(None, "gx"),
        P(None, "gx"),
        P(None, "gx"),
        P(None, "gx"),
        P("gx", None),
    )
    out_specs = P(("groups", "gx"), None)

    def layer(tokens, *rest):
        size = mesh.shape["gx"]
        width, units = tokens.shape[1], rest[-3].shape[1] // size
        fits = size == 16 and units == 2 * CHUNK and width == PER * CHUNK
        body = four_by_two if fits else any_size
        whole = jax.shard_map(body, mesh=mesh, in_specs=in_specs, out_specs=out_specs, check_vma=False)
        return whole(tokens, *rest)

    return layer
```

```python
import functools

import jax
import jax.numpy as jnp
from jax import lax
from jax.experimental import pallas as pl
from jax.experimental.pallas import tpu as pltpu
from jax.sharding import PartitionSpec as P

EH = 4096
CHUNK = 1024
PER = 7
SLOTS = 4
AHEAD = (1, 0, 0, 0, 0)
MIB = 1 << 20

VMEM = pl.BlockSpec(memory_space=pltpu.VMEM)
SMEM = pl.BlockSpec(memory_space=pltpu.SMEM)
ANY = pl.BlockSpec(memory_space=pl.ANY)


def in_hbm(x):
    return pltpu.with_memory_space_constraint(x, pltpu.HBM)


def in_vmem(x):
    return pltpu.with_memory_space_constraint(x, pltpu.VMEM)


def cost(flops, moved):
    return pl.CostEstimate(flops=flops, bytes_accessed=moved, transcendentals=0)


def limit(mib):
    return pltpu.CompilerParams(vmem_limit_bytes=mib * MIB)


def dot(x, w):
    return jnp.dot(x, w, preferred_element_type=jnp.float32)


def dot_t(x, w):
    return lax.dot_general(x, w, (((1,), (1,)), ((), ())), preferred_element_type=jnp.float32)


def swiglu_hidden(gate, upward):
    return (jax.nn.silu(gate) * upward).astype(jnp.bfloat16)


def tokens_at(shape, axis, owned):
    p = lax.broadcasted_iota(jnp.int32, shape, axis)
    block, row = p // owned, p % owned
    step = (block & 3) * 4 + ((block >> 2) & 1) * 2 + ((block >> 3) & 1)
    return (lax.axis_index("gx") ^ step) * owned + row


def swap_matrix(rows, owned, to_tokens):
    shape = (rows, rows)
    token = lax.broadcasted_iota(jnp.int32, shape, 0 if to_tokens else 1)
    held = tokens_at(shape, 1 if to_tokens else 0, owned)
    return jnp.where(token == held, 1.0, 0.0).astype(jnp.bfloat16)


def chunk_source(chunk, gate_ref, up_ref):
    source = gate_ref if chunk < PER else up_ref
    return source.at[pl.ds(chunk % PER * CHUNK, CHUNK)]


def start_copies(pairs, sems):
    copies = [pltpu.make_async_copy(source, target, sems.at[n]) for n, (source, target) in enumerate(pairs)]
    for copy in copies:
        copy.start()
    return copies


def wait_copies(copies):
    for copy in copies:
        copy.wait()


def chunk_shapes(count):
    return [pltpu.VMEM((CHUNK, 2 * CHUNK), jnp.bfloat16)] * count


def fetch_kernel(chunks, whole_count, tied, *refs):
    refs = refs[1:] if tied else refs
    gate_ref, up_ref, refs = refs[0], refs[1], refs[2:]
    wholes, refs = refs[:whole_count], refs[whole_count:]
    count = len(chunks)
    held, targets, (done_ref, sems) = refs[:count], refs[count : count + whole_count], refs[count + whole_count :]
    pairs = [(chunk_source(c, gate_ref, up_ref), ref) for c, ref in zip(chunks, held)]
    copies = start_copies(pairs + list(zip(wholes, targets)), sems)
    done_ref[...] = jnp.zeros_like(done_ref)
    wait_copies(copies)


def fetch(after, chunks, gate, up, *wholes):
    tied = after is not None
    count = len(chunks)
    found = pl.pallas_call(
        functools.partial(fetch_kernel, chunks, len(wholes), tied),
        out_shape=(
            *chunk_shapes(count),
            *[pltpu.VMEM(w.shape, w.dtype) for w in wholes],
            pltpu.VMEM((8, 128), jnp.float32),
        ),
        in_specs=[VMEM] * tied + [ANY] * (2 + len(wholes)),
        out_specs=(VMEM,) * (count + len(wholes) + 1),
        scratch_shapes=[pltpu.SemaphoreType.DMA((count + len(wholes),))],
        cost_estimate=cost(0, 4 * count * CHUNK * CHUNK + sum(2 * w.size for w in wholes)),
        compiler_params=limit(1),
    )(*([in_vmem(after)] if tied else []), in_hbm(gate), in_hbm(up), *[in_hbm(w) for w in wholes])
    return list(found[:count]), *found[count:]


def join_kernel(count, *refs):
    blocks, joined = refs[-1 - count : -1], refs[-1]
    at = 0
    for block in blocks:
        size = block.shape[0]
        joined[at : at + size] = block[...]
        at += size


def join(done, *blocks):
    shape = (sum(b.shape[0] for b in blocks),) + blocks[0].shape[1:]
    ties = [] if done is None else [in_vmem(done)]
    return pl.pallas_call(
        functools.partial(join_kernel, len(blocks)),
        out_shape=pltpu.VMEM(shape, blocks[0].dtype),
        in_specs=[VMEM] * (len(ties) + len(blocks)),
        out_specs=VMEM,
        cost_estimate=cost(0, 4 * sum(b.size for b in blocks)),
        compiler_params=limit(4),
    )(*ties, *blocks)


def dense_in_kernel(
    owned, chunks, mine_ref, other_ref, dense_gate, dense_up, gate_ref, up_ref, hidden_ref, x_ref, *refs
):
    held, sems = refs[:-1], refs[-1]
    copies = start_copies([(chunk_source(c, gate_ref, up_ref), ref) for c, ref in zip(chunks, held)], sems)
    half = mine_ref.shape[0]
    x_ref[0:half] = mine_ref[...]
    x_ref[half : 2 * half] = other_ref[...]
    hidden = swiglu_hidden(dot_t(x_ref[...], dense_gate[...]), dot_t(x_ref[...], dense_up[...]))
    hidden_ref[0] = dot(swap_matrix(2 * half, owned, True), hidden).astype(jnp.bfloat16)
    wait_copies(copies)


def dense_in(owned, chunks, mine, other, dense_gate, dense_up, gate, up):
    rows, width = 2 * mine.shape[0], mine.shape[1]
    count = len(chunks)
    hidden, x, *held = pl.pallas_call(
        functools.partial(dense_in_kernel, owned, chunks),
        out_shape=(
            pltpu.VMEM((1, rows, dense_gate.shape[0]), jnp.bfloat16),
            pltpu.VMEM((rows, width), jnp.bfloat16),
            *chunk_shapes(count),
        ),
        in_specs=[VMEM] * 4 + [ANY] * 2,
        out_specs=(VMEM,) * (2 + count),
        scratch_shapes=[pltpu.SemaphoreType.DMA((max(count, 1),))],
        cost_estimate=cost(4 * rows * dense_gate.size, 4 * dense_gate.size),
        compiler_params=limit(4),
    )(in_vmem(mine), other, in_vmem(dense_gate), in_vmem(dense_up), in_hbm(gate), in_hbm(up))
    return hidden, x, held


def expert_kernel(owned, there, x_ref, ids_ref, gates_ref, gate_ref, *refs):
    ready = [gate_ref.at[pl.ds(n * CHUNK, CHUNK)] for n in range(PER)] + list(refs[:there])
    refs = refs[there:]
    there += PER
    up_ref, down_ref, out_ref, gate_sum, up_sum, hidden, ring, sems = refs
    rows, units = gate_sum.shape
    slots = ring.shape[0]
    blocks = PER // 2
    pieces = [[(chunk_source(c, gate_ref, up_ref), 0)] for c in range(there, 2 * PER)]
    streamed = len(pieces)
    for block in range(blocks):
        for part in range(2):
            held = down_ref.at[pl.ds(part * CHUNK, CHUNK), pl.ds(block * units, units)]
            pieces.append([(held, 0)])
    parts = [down_ref.at[pl.ds(part * CHUNK, CHUNK), pl.ds(blocks * units, CHUNK)] for part in range(2)]
    pieces.append([(parts[0], 0), (parts[1], CHUNK)])
    total = len(pieces)
    found = {}

    def issue(n):
        if n < total:
            found[n] = []
            for source, column in pieces[n]:
                slot = ring.at[n % slots]
                target = slot if len(pieces[n]) == 1 else slot.at[:, pl.ds(column, CHUNK)]
                copy = pltpu.make_async_copy(source, target, sems.at[slots if column else n % slots])
                copy.start()
                found[n].append(copy)

    def arrived(n):
        wait_copies(found[n])
        return ring.at[n % slots]

    for n in range(slots):
        issue(n)

    begun = set()

    def add(chunk, weights):
        target = gate_sum if chunk < PER else up_sum
        at = chunk % PER * CHUNK
        product = dot(x_ref[:, at : at + CHUNK], weights[...])
        target[...] = target[...] + product if chunk // PER in begun else product
        begun.add(chunk // PER)

    lead = max(there - streamed, 1)
    for n in range(lead):
        add(n, ready[n])
    for n in range(max(there - lead, streamed)):
        if n < streamed:
            add(there + n, arrived(n))
            issue(n + slots)
        if lead + n < there:
            add(lead + n, ready[lead + n])
    hidden[...] = swiglu_hidden(gate_sum[...], up_sum[...])

    expert = lax.axis_index("gx") * units // EH
    weights = jnp.sum(jnp.where(ids_ref[...] == expert, gates_ref[...], 0.0), axis=0, keepdims=True)
    token = lax.broadcasted_iota(jnp.int32, (rows, rows), 1)
    scale = jnp.sum(jnp.where(token == tokens_at((rows, rows), 0, owned), weights, 0.0), axis=1, keepdims=True)

    first, second = hidden[:, 0:CHUNK], hidden[:, CHUNK : 2 * CHUNK]
    for block in range(blocks):
        n = streamed + 2 * block
        at = pl.ds(block * units, units)
        out_ref[:, at] = dot(first, arrived(n)[...])
        issue(n + slots)
        out_ref[:, at] = scale * (out_ref[:, at] + dot(second, arrived(n + 1)[...]))
        issue(n + 1 + slots)
    last = arrived(total - 1)
    both = dot(first, last[:, 0:CHUNK]) + dot(second, last[:, CHUNK : 2 * CHUNK])
    out_ref[:, blocks * units :] = scale * both


def expert_block(owned, x, ids, gates, ready, gate, up, down):
    rows, width = x.shape
    units = gate.shape[1]
    return pl.pallas_call(
        functools.partial(expert_kernel, owned, len(ready)),
        out_shape=pltpu.VMEM((rows, width), jnp.float32),
        in_specs=[VMEM] * (4 + len(ready)) + [ANY] * 2,
        out_specs=VMEM,
        scratch_shapes=[
            pltpu.VMEM((rows, units), jnp.float32),
            pltpu.VMEM((rows, units), jnp.float32),
            pltpu.VMEM((rows, units), jnp.bfloat16),
            pltpu.VMEM((SLOTS, CHUNK, units), jnp.bfloat16),
            pltpu.SemaphoreType.DMA((SLOTS + 1,)),
        ],
        cost_estimate=cost(6 * rows * down.size, 4 * down.size),
        compiler_params=limit(4 * SLOTS + 3),
    )(
        in_vmem(x), ids, gates, in_vmem(gate), *[in_vmem(r) for r in ready],
        in_hbm(up), in_hbm(down),
    )


def dense_out_kernel(owned, part_ref, b0, b1, b2, b3, down_ref, keep_ref, send_ref, held, joined, wide):
    near, rows, units = b0.shape
    half = rows // 2
    columns, width = down_ref.shape[0], part_ref.shape[1]
    own = lax.axis_index("gx")
    for z, blocks in enumerate((b0, b1, b2, b3)):
        held[z * near : (z + 1) * near] = blocks[...]
    for j in range(4 * near):
        joined[:, j * units : (j + 1) * units] = held[own ^ j]
    dense_rows = dot(swap_matrix(rows, owned, False), joined[...]).astype(jnp.bfloat16)
    wide[...] = jnp.zeros_like(wide)
    wide[:, 0:columns] = dot_t(dense_rows, down_ref[...])
    start = own * columns
    base = jnp.minimum(start // 128 * 128, width - wide.shape[1])
    moved = pltpu.roll(wide[...], start - base, 1)
    at = pl.ds(pl.multiple_of(base, 128), wide.shape[1])
    keep_ref[...] = part_ref[0:half]
    send_ref[...] = part_ref[half:].astype(jnp.bfloat16)
    keep_ref[:, at] += moved[:half]
    send_ref[:, at] = (part_ref[half:, at] + moved[half:]).astype(jnp.bfloat16)


def dense_out(owned, part, blocks, down):
    near, rows, units = blocks[0].shape
    columns, inner = down.shape
    width = part.shape[1]
    window = -(-(columns + 64) // 128) * 128 if columns % 64 == 0 else -(-(columns + 127) // 128) * 128
    return pl.pallas_call(
        functools.partial(dense_out_kernel, owned),
        out_shape=(
            jax.ShapeDtypeStruct((rows // 2, width), jnp.float32),
            jax.ShapeDtypeStruct((rows // 2, width), jnp.bfloat16),
        ),
        in_specs=[VMEM] * 6,
        out_specs=(VMEM, VMEM),
        scratch_shapes=[
            pltpu.VMEM((4 * near, rows, units), jnp.bfloat16),
            pltpu.VMEM((rows, inner), jnp.bfloat16),
            pltpu.VMEM((rows, window), jnp.float32),
        ],
        cost_estimate=cost(2 * rows * down.size, 2 * down.size),
        compiler_params=limit(8),
    )(in_vmem(part), *blocks, in_vmem(down))


def four_by_two(
    tokens,
    route_ids,
    route_gates,
    dense_gate,
    dense_up,
    dense_down,
    expert_gate,
    expert_up,
    expert_down,
):
    owned, width = tokens.shape
    dense_gate, dense_up, dense_down = dense_gate.T, dense_up.T, dense_down.T

    def swap(value, step):
        return lax.ppermute(value, "gx", [(i, i ^ step) for i in range(16)])

    ends = [sum(AHEAD[: n + 1]) for n in range(len(AHEAD))]
    chunks = [range(PER + end - count, PER + end) for count, end in zip(AHEAD, ends)]
    streams = (expert_gate, expert_up)
    along_z = [swap(tokens, 4 * z) for z in (1, 2, 3)]
    ready, done = [], None
    if AHEAD[0]:
        ready, done = fetch(None, chunks[0], *streams)
    mine = join(done, tokens, *along_z)
    along_x = swap(mine, 2)
    if AHEAD[1]:
        more, done = fetch(done, chunks[1], *streams)
        ready += more
    mine = join(done, mine, along_x)
    other = swap(mine, 1)
    if AHEAD[2]:
        more, _ = fetch(done, chunks[2], *streams)
        ready += more

    block, x, more = dense_in(owned, chunks[3], mine, other, dense_gate, dense_up, *streams)
    ready += more
    near = [block] + [swap(block, step) for step in (1, 2, 3)]
    if AHEAD[4]:
        more, done = fetch(block, chunks[4], *streams)
        ready += more
    else:
        done = None
    block = join(done, *near)
    blocks = [block] + [swap(block, 4 * z) for z in (1, 2, 3)]
    part = expert_block(owned, x, route_ids.T, route_gates.T, ready, expert_gate, expert_up, expert_down)
    keep, send = dense_out(owned, part, blocks, dense_down)

    half = keep.shape[0] // 2
    keep = keep + swap(send, 1).astype(jnp.float32)
    keep = keep[:half] + swap(keep[half:].astype(jnp.bfloat16), 2).astype(jnp.float32)
    rest = keep.astype(jnp.bfloat16)
    total = tokens.astype(jnp.float32) + keep[:owned]
    for z in (1, 2, 3):
        total = total + swap(rest[z * owned : (z + 1) * owned], 4 * z).astype(jnp.float32)
    return total.astype(jnp.bfloat16)


def swiglu(row_block, w_gate, w_up, w_down):
    gate = jnp.dot(row_block, w_gate, preferred_element_type=jnp.float32)
    upward = jnp.dot(row_block, w_up, preferred_element_type=jnp.float32)
    hidden = (jax.nn.silu(gate) * upward).astype(jnp.bfloat16)
    return jnp.dot(hidden, w_down, preferred_element_type=jnp.float32)


def any_size(
    tokens,
    route_ids,
    route_gates,
    dense_gate,
    dense_up,
    dense_down,
    expert_gate,
    expert_up,
    expert_down,
):
    gathered = lax.all_gather(tokens, "gx", axis=0, tiled=True)
    total_rows = gathered.shape[0]
    model_width = gathered.shape[1]
    own_index = lax.axis_index("gx")
    gate = jnp.dot(gathered, dense_gate, preferred_element_type=jnp.float32)
    upward = jnp.dot(gathered, dense_up, preferred_element_type=jnp.float32)
    dense_hidden = (jax.nn.silu(gate) * upward).astype(jnp.bfloat16)
    dense_part = jnp.dot(
        lax.all_gather(dense_hidden, "gx", axis=1, tiled=True),
        dense_down,
        preferred_element_type=jnp.float32,
    )
    slice_width = expert_gate.shape[1]
    expert = own_index * slice_width // EH
    flat_ids = route_ids.reshape(-1)
    flat_gates = route_gates.reshape(-1)
    matches = flat_ids == expert
    position = jnp.cumsum(matches.astype(jnp.int32)) - 1
    target = jnp.where(matches, position, total_rows)
    source_row = jnp.arange(flat_ids.shape[0], dtype=jnp.int32) // route_ids.shape[1]
    slot_rows = jnp.zeros((total_rows,), jnp.int32).at[target].set(source_row, mode="drop")
    slot_weights = jnp.zeros((total_rows,), jnp.float32).at[target].set(flat_gates, mode="drop")
    picked = gathered[slot_rows]
    slot_out = swiglu(picked, expert_gate, expert_up, expert_down)
    weighted = slot_weights[:, None] * slot_out
    expert_term = jnp.zeros((total_rows, model_width), jnp.float32).at[slot_rows].add(weighted)
    moe_rows = lax.psum_scatter(expert_term, "gx", scatter_dimension=0, tiled=True)
    dense_rows = lax.all_to_all(dense_part, "gx", split_axis=0, concat_axis=1, tiled=True)
    result = tokens.astype(jnp.float32) + dense_rows + moe_rows
    return result.astype(jnp.bfloat16)


def solution(mesh):
    in_specs = (
        P(("groups", "gx"), None),
        P("groups", None),
        P("groups", None),
        P(None, "gx"),
        P(None, "gx"),
        P(None, "gx"),
        P(None, "gx"),
        P(None, "gx"),
        P("gx", None),
    )
    out_specs = P(("groups", "gx"), None)

    def layer(tokens, *rest):
        size = mesh.shape["gx"]
        width, units = tokens.shape[1], rest[-3].shape[1] // size
        fits = size == 16 and units == 2 * CHUNK and width == PER * CHUNK
        body = four_by_two if fits else any_size
        whole = jax.shard_map(body, mesh=mesh, in_specs=in_specs, out_specs=out_specs, check_vma=False)
        return whole(tokens, *rest)

    return layer
```

```python
import functools

import jax
import jax.numpy as jnp
from jax import lax
from jax.experimental import pallas as pl
from jax.experimental.pallas import tpu as pltpu
from jax.sharding import PartitionSpec as P

EH = 4096
CHUNK = 1024
PER = 7
SLOTS = 4
AHEAD = (1, 0, 0, 0, 0)
MIB = 1 << 20

VMEM = pl.BlockSpec(memory_space=pltpu.VMEM)
SMEM = pl.BlockSpec(memory_space=pltpu.SMEM)
ANY = pl.BlockSpec(memory_space=pl.ANY)


def in_hbm(x):
    return pltpu.with_memory_space_constraint(x, pltpu.HBM)


def in_vmem(x):
    return pltpu.with_memory_space_constraint(x, pltpu.VMEM)


def cost(flops, moved):
    return pl.CostEstimate(flops=flops, bytes_accessed=moved, transcendentals=0)


def limit(mib):
    return pltpu.CompilerParams(vmem_limit_bytes=mib * MIB)


def dot(x, w):
    return jnp.dot(x, w, preferred_element_type=jnp.float32)


def dot_t(x, w):
    return lax.dot_general(x, w, (((1,), (1,)), ((), ())), preferred_element_type=jnp.float32)


def swiglu_hidden(gate, upward):
    return (jax.nn.silu(gate) * upward).astype(jnp.bfloat16)


def tokens_at(shape, axis, owned):
    p = lax.broadcasted_iota(jnp.int32, shape, axis)
    block, row = p // owned, p % owned
    step = (block & 3) * 4 + ((block >> 2) & 1) * 2 + ((block >> 3) & 1)
    return (lax.axis_index("gx") ^ step) * owned + row


def swap_matrix(rows, owned, to_tokens):
    shape = (rows, rows)
    token = lax.broadcasted_iota(jnp.int32, shape, 0 if to_tokens else 1)
    held = tokens_at(shape, 1 if to_tokens else 0, owned)
    return jnp.where(token == held, 1.0, 0.0).astype(jnp.bfloat16)


def chunk_source(chunk, gate_ref, up_ref):
    source = gate_ref if chunk < PER else up_ref
    return source.at[pl.ds(chunk % PER * CHUNK, CHUNK)]


def start_copies(pairs, sems):
    copies = [pltpu.make_async_copy(source, target, sems.at[n]) for n, (source, target) in enumerate(pairs)]
    for copy in copies:
        copy.start()
    return copies


def wait_copies(copies):
    for copy in copies:
        copy.wait()


def chunk_shapes(count):
    return [pltpu.VMEM((CHUNK, 2 * CHUNK), jnp.bfloat16)] * count


def fetch_kernel(chunks, whole_count, tied, *refs):
    refs = refs[1:] if tied else refs
    gate_ref, up_ref, refs = refs[0], refs[1], refs[2:]
    wholes, refs = refs[:whole_count], refs[whole_count:]
    count = len(chunks)
    held, targets, (done_ref, sems) = refs[:count], refs[count : count + whole_count], refs[count + whole_count :]
    pairs = [(chunk_source(c, gate_ref, up_ref), ref) for c, ref in zip(chunks, held)]
    copies = start_copies(pairs + list(zip(wholes, targets)), sems)
    done_ref[...] = jnp.zeros_like(done_ref)
    wait_copies(copies)


def fetch(after, chunks, gate, up, *wholes):
    tied = after is not None
    count = len(chunks)
    found = pl.pallas_call(
        functools.partial(fetch_kernel, chunks, len(wholes), tied),
        out_shape=(
            *chunk_shapes(count),
            *[pltpu.VMEM(w.shape, w.dtype) for w in wholes],
            pltpu.VMEM((8, 128), jnp.float32),
        ),
        in_specs=[VMEM] * tied + [ANY] * (2 + len(wholes)),
        out_specs=(VMEM,) * (count + len(wholes) + 1),
        scratch_shapes=[pltpu.SemaphoreType.DMA((count + len(wholes),))],
        cost_estimate=cost(0, 4 * count * CHUNK * CHUNK + sum(2 * w.size for w in wholes)),
        compiler_params=limit(1),
    )(*([in_vmem(after)] if tied else []), in_hbm(gate), in_hbm(up), *[in_hbm(w) for w in wholes])
    return list(found[:count]), *found[count:]


def join_kernel(count, *refs):
    blocks, joined = refs[-1 - count : -1], refs[-1]
    at = 0
    for block in blocks:
        size = block.shape[0]
        joined[at : at + size] = block[...]
        at += size


def join(done, *blocks):
    shape = (sum(b.shape[0] for b in blocks),) + blocks[0].shape[1:]
    ties = [] if done is None else [in_vmem(done)]
    return pl.pallas_call(
        functools.partial(join_kernel, len(blocks)),
        out_shape=pltpu.VMEM(shape, blocks[0].dtype),
        in_specs=[VMEM] * (len(ties) + len(blocks)),
        out_specs=VMEM,
        cost_estimate=cost(0, 4 * sum(b.size for b in blocks)),
        compiler_params=limit(4),
    )(*ties, *blocks)


def dense_in_kernel(
    owned, chunks, mine_ref, other_ref, dense_gate, dense_up, gate_ref, up_ref, hidden_ref, x_ref, *refs
):
    held, sems = refs[:-1], refs[-1]
    copies = start_copies([(chunk_source(c, gate_ref, up_ref), ref) for c, ref in zip(chunks, held)], sems)
    half = mine_ref.shape[0]
    x_ref[0:half] = mine_ref[...]
    x_ref[half : 2 * half] = other_ref[...]
    hidden = swiglu_hidden(dot_t(x_ref[...], dense_gate[...]), dot_t(x_ref[...], dense_up[...]))
    hidden_ref[0] = dot(swap_matrix(2 * half, owned, True), hidden).astype(jnp.bfloat16)
    wait_copies(copies)


def dense_in(owned, chunks, mine, other, dense_gate, dense_up, gate, up):
    rows, width = 2 * mine.shape[0], mine.shape[1]
    count = len(chunks)
    hidden, x, *held = pl.pallas_call(
        functools.partial(dense_in_kernel, owned, chunks),
        out_shape=(
            pltpu.VMEM((1, rows, dense_gate.shape[0]), jnp.bfloat16),
            pltpu.VMEM((rows, width), jnp.bfloat16),
            *chunk_shapes(count),
        ),
        in_specs=[VMEM] * 4 + [ANY] * 2,
        out_specs=(VMEM,) * (2 + count),
        scratch_shapes=[pltpu.SemaphoreType.DMA((max(count, 1),))],
        cost_estimate=cost(4 * rows * dense_gate.size, 4 * dense_gate.size),
        compiler_params=limit(4),
    )(in_vmem(mine), other, in_vmem(dense_gate), in_vmem(dense_up), in_hbm(gate), in_hbm(up))
    return hidden, x, held


def expert_kernel(owned, there, x_ref, ids_ref, gates_ref, gate_ref, *refs):
    ready = [gate_ref.at[pl.ds(n * CHUNK, CHUNK)] for n in range(PER)] + list(refs[:there])
    refs = refs[there:]
    there += PER
    up_ref, down_ref, out_ref, gate_sum, up_sum, hidden, ring, sems = refs
    rows, units = gate_sum.shape
    slots = ring.shape[0]
    blocks = PER // 2
    pieces = [[(chunk_source(c, gate_ref, up_ref), 0)] for c in range(there, 2 * PER)]
    streamed = len(pieces)
    for block in range(blocks):
        for part in range(2):
            held = down_ref.at[pl.ds(part * CHUNK, CHUNK), pl.ds(block * units, units)]
            pieces.append([(held, 0)])
    parts = [down_ref.at[pl.ds(part * CHUNK, CHUNK), pl.ds(blocks * units, CHUNK)] for part in range(2)]
    pieces.append([(parts[0], 0), (parts[1], CHUNK)])
    total = len(pieces)
    found = {}

    def issue(n):
        if n < total:
            found[n] = []
            for source, column in pieces[n]:
                slot = ring.at[n % slots]
                target = slot if len(pieces[n]) == 1 else slot.at[:, pl.ds(column, CHUNK)]
                copy = pltpu.make_async_copy(source, target, sems.at[slots if column else n % slots])
                copy.start()
                found[n].append(copy)

    def arrived(n):
        wait_copies(found[n])
        return ring.at[n % slots]

    for n in range(slots):
        issue(n)

    begun = set()

    def add(chunk, weights):
        target = gate_sum if chunk < PER else up_sum
        at = chunk % PER * CHUNK
        product = dot(x_ref[:, at : at + CHUNK], weights[...])
        target[...] = target[...] + product if chunk // PER in begun else product
        begun.add(chunk // PER)

    lead = max(there - streamed, 1)
    for n in range(lead):
        add(n, ready[n])
    for n in range(max(there - lead, streamed)):
        if n < streamed:
            add(there + n, arrived(n))
            issue(n + slots)
        if lead + n < there:
            add(lead + n, ready[lead + n])
    hidden[...] = swiglu_hidden(gate_sum[...], up_sum[...])

    expert = lax.axis_index("gx") * units // EH
    weights = jnp.sum(jnp.where(ids_ref[...] == expert, gates_ref[...], 0.0), axis=0, keepdims=True)
    token = lax.broadcasted_iota(jnp.int32, (rows, rows), 1)
    scale = jnp.sum(jnp.where(token == tokens_at((rows, rows), 0, owned), weights, 0.0), axis=1, keepdims=True)

    first, second = hidden[:, 0:CHUNK], hidden[:, CHUNK : 2 * CHUNK]
    for block in range(blocks):
        n = streamed + 2 * block
        at = pl.ds(block * units, units)
        out_ref[:, at] = dot(first, arrived(n)[...])
        issue(n + slots)
        out_ref[:, at] = scale * (out_ref[:, at] + dot(second, arrived(n + 1)[...]))
        issue(n + 1 + slots)
    last = arrived(total - 1)
    both = dot(first, last[:, 0:CHUNK]) + dot(second, last[:, CHUNK : 2 * CHUNK])
    out_ref[:, blocks * units :] = scale * both


def expert_block(owned, x, ids, gates, ready, gate, up, down):
    rows, width = x.shape
    units = gate.shape[1]
    return pl.pallas_call(
        functools.partial(expert_kernel, owned, len(ready)),
        out_shape=pltpu.VMEM((rows, width), jnp.float32),
        in_specs=[VMEM] * (4 + len(ready)) + [ANY] * 2,
        out_specs=VMEM,
        scratch_shapes=[
            pltpu.VMEM((rows, units), jnp.float32),
            pltpu.VMEM((rows, units), jnp.float32),
            pltpu.VMEM((rows, units), jnp.bfloat16),
            pltpu.VMEM((SLOTS, CHUNK, units), jnp.bfloat16),
            pltpu.SemaphoreType.DMA((SLOTS + 1,)),
        ],
        cost_estimate=cost(6 * rows * down.size, 4 * down.size),
        compiler_params=limit(4 * SLOTS + 3),
    )(
        in_vmem(x), ids, gates, in_vmem(gate), *[in_vmem(r) for r in ready],
        in_hbm(up), in_hbm(down),
    )


def dense_out_kernel(owned, part_ref, b0, b1, b2, b3, down_ref, keep_ref, send_ref, held, joined, wide):
    near, rows, units = b0.shape
    half = rows // 2
    columns, width = down_ref.shape[0], part_ref.shape[1]
    own = lax.axis_index("gx")
    for z, blocks in enumerate((b0, b1, b2, b3)):
        held[z * near : (z + 1) * near] = blocks[...]
    for j in range(4 * near):
        joined[:, j * units : (j + 1) * units] = held[own ^ j]
    wide[...] = jnp.zeros_like(wide)
    wide[:, 0:columns] = dot_t(joined[...], down_ref[...])
    order = swap_matrix(rows, owned, False).astype(jnp.float32)
    wide[...] = jnp.dot(order, wide[...], precision=lax.Precision.HIGHEST, preferred_element_type=jnp.float32)
    start = own * columns
    base = jnp.minimum(start // 128 * 128, width - wide.shape[1])
    moved = pltpu.roll(wide[...], start - base, 1)
    at = pl.ds(pl.multiple_of(base, 128), wide.shape[1])
    keep_ref[...] = part_ref[0:half]
    send_ref[...] = part_ref[half:].astype(jnp.bfloat16)
    keep_ref[:, at] += moved[:half]
    send_ref[:, at] = (part_ref[half:, at] + moved[half:]).astype(jnp.bfloat16)


def dense_out(owned, part, blocks, down):
    near, rows, units = blocks[0].shape
    columns, inner = down.shape
    width = part.shape[1]
    window = -(-(columns + 64) // 128) * 128 if columns % 64 == 0 else -(-(columns + 127) // 128) * 128
    return pl.pallas_call(
        functools.partial(dense_out_kernel, owned),
        out_shape=(
            jax.ShapeDtypeStruct((rows // 2, width), jnp.float32),
            jax.ShapeDtypeStruct((rows // 2, width), jnp.bfloat16),
        ),
        in_specs=[VMEM] * 6,
        out_specs=(VMEM, VMEM),
        scratch_shapes=[
            pltpu.VMEM((4 * near, rows, units), jnp.bfloat16),
            pltpu.VMEM((rows, inner), jnp.bfloat16),
            pltpu.VMEM((rows, window), jnp.float32),
        ],
        cost_estimate=cost(2 * rows * down.size, 2 * down.size),
        compiler_params=limit(8),
    )(in_vmem(part), *blocks, in_vmem(down))


def four_by_two(
    tokens,
    route_ids,
    route_gates,
    dense_gate,
    dense_up,
    dense_down,
    expert_gate,
    expert_up,
    expert_down,
):
    owned, width = tokens.shape
    dense_gate, dense_up, dense_down = dense_gate.T, dense_up.T, dense_down.T

    def swap(value, step):
        return lax.ppermute(value, "gx", [(i, i ^ step) for i in range(16)])

    ends = [sum(AHEAD[: n + 1]) for n in range(len(AHEAD))]
    chunks = [range(PER + end - count, PER + end) for count, end in zip(AHEAD, ends)]
    streams = (expert_gate, expert_up)
    along_z = [swap(tokens, 4 * z) for z in (1, 2, 3)]
    ready, done = [], None
    if AHEAD[0]:
        ready, done = fetch(None, chunks[0], *streams)
    mine = join(done, tokens, *along_z)
    along_x = swap(mine, 2)
    if AHEAD[1]:
        more, done = fetch(done, chunks[1], *streams)
        ready += more
    mine = join(done, mine, along_x)
    other = swap(mine, 1)
    if AHEAD[2]:
        more, _ = fetch(done, chunks[2], *streams)
        ready += more

    block, x, more = dense_in(owned, chunks[3], mine, other, dense_gate, dense_up, *streams)
    ready += more
    near = [block] + [swap(block, step) for step in (1, 2, 3)]
    if AHEAD[4]:
        more, done = fetch(block, chunks[4], *streams)
        ready += more
    else:
        done = None
    block = join(done, *near)
    blocks = [block] + [swap(block, 4 * z) for z in (1, 2, 3)]
    part = expert_block(owned, x, route_ids.T, route_gates.T, ready, expert_gate, expert_up, expert_down)
    keep, send = dense_out(owned, part, blocks, dense_down)

    half = keep.shape[0] // 2
    keep = keep + swap(send, 1).astype(jnp.float32)
    keep = keep[:half] + swap(keep[half:].astype(jnp.bfloat16), 2).astype(jnp.float32)
    rest = keep.astype(jnp.bfloat16)
    total = tokens.astype(jnp.float32) + keep[:owned]
    for z in (1, 2, 3):
        total = total + swap(rest[z * owned : (z + 1) * owned], 4 * z).astype(jnp.float32)
    return total.astype(jnp.bfloat16)


def swiglu(row_block, w_gate, w_up, w_down):
    gate = jnp.dot(row_block, w_gate, preferred_element_type=jnp.float32)
    upward = jnp.dot(row_block, w_up, preferred_element_type=jnp.float32)
    hidden = (jax.nn.silu(gate) * upward).astype(jnp.bfloat16)
    return jnp.dot(hidden, w_down, preferred_element_type=jnp.float32)


def any_size(
    tokens,
    route_ids,
    route_gates,
    dense_gate,
    dense_up,
    dense_down,
    expert_gate,
    expert_up,
    expert_down,
):
    gathered = lax.all_gather(tokens, "gx", axis=0, tiled=True)
    total_rows = gathered.shape[0]
    model_width = gathered.shape[1]
    own_index = lax.axis_index("gx")
    gate = jnp.dot(gathered, dense_gate, preferred_element_type=jnp.float32)
    upward = jnp.dot(gathered, dense_up, preferred_element_type=jnp.float32)
    dense_hidden = (jax.nn.silu(gate) * upward).astype(jnp.bfloat16)
    dense_part = jnp.dot(
        lax.all_gather(dense_hidden, "gx", axis=1, tiled=True),
        dense_down,
        preferred_element_type=jnp.float32,
    )
    slice_width = expert_gate.shape[1]
    expert = own_index * slice_width // EH
    flat_ids = route_ids.reshape(-1)
    flat_gates = route_gates.reshape(-1)
    matches = flat_ids == expert
    position = jnp.cumsum(matches.astype(jnp.int32)) - 1
    target = jnp.where(matches, position, total_rows)
    source_row = jnp.arange(flat_ids.shape[0], dtype=jnp.int32) // route_ids.shape[1]
    slot_rows = jnp.zeros((total_rows,), jnp.int32).at[target].set(source_row, mode="drop")
    slot_weights = jnp.zeros((total_rows,), jnp.float32).at[target].set(flat_gates, mode="drop")
    picked = gathered[slot_rows]
    slot_out = swiglu(picked, expert_gate, expert_up, expert_down)
    weighted = slot_weights[:, None] * slot_out
    expert_term = jnp.zeros((total_rows, model_width), jnp.float32).at[slot_rows].add(weighted)
    moe_rows = lax.psum_scatter(expert_term, "gx", scatter_dimension=0, tiled=True)
    dense_rows = lax.all_to_all(dense_part, "gx", split_axis=0, concat_axis=1, tiled=True)
    result = tokens.astype(jnp.float32) + dense_rows + moe_rows
    return result.astype(jnp.bfloat16)


def solution(mesh):
    in_specs = (
        P(("groups", "gx"), None),
        P("groups", None),
        P("groups", None),
        P(None, "gx"),
        P(None, "gx"),
        P(None, "gx"),
        P(None, "gx"),
        P(None, "gx"),
        P("gx", None),
    )
    out_specs = P(("groups", "gx"), None)

    def layer(tokens, *rest):
        size = mesh.shape["gx"]
        width, units = tokens.shape[1], rest[-3].shape[1] // size
        fits = size == 16 and units == 2 * CHUNK and width == PER * CHUNK
        body = four_by_two if fits else any_size
        whole = jax.shard_map(body, mesh=mesh, in_specs=in_specs, out_specs=out_specs, check_vma=False)
        return whole(tokens, *rest)

    return layer
```
